512 devices in a mesh: group: 4 (over x_lo, core), dp: 8 (over y), tensor: 16 (over z, x_hi).
Axes of the slice: x: 4 (x_hi: 2, x_lo: 2; x = x_hi * 2 + x_lo), y: 8, z: 8, core: 2. Of those that a mesh axis runs over, the one named last changes fastest.
Arguments:
- activations: bfloat16 [24576, 5120], P(('group', 'dp'), 'tensor'), may hold values from -6 to 6
- norm_gain: float32 [5120], replicated, may hold values from 0.5 to 1.5
- master_weight: float32 [5120, 16, 3, 128], P(('group', 'dp'), 'tensor'), may hold values from -0.078125 to 0.078125
- grad: bfloat16 [5120, 16, 3, 128], P(('group', 'dp'), 'tensor'), may hold values from -12 to 12
- moment: float32 [5120, 16, 3, 128], P(('group', 'dp'), 'tensor'), may hold values from -0.0024414062 to 0.0024414062
- variance: float32 [5120, 16, 3, 128], P(('group', 'dp'), 'tensor'), may hold values from 1.5894572e-09 to 6.357829e-08
- query_gain: float32 [32, 128], P('tensor'), may hold values from 1 to 2.5
- key_gain: float32 [8, 128], replicated, may hold values from 1 to 2.5
- prompt_len: int32 [32], P(('group', 'dp')), may hold values from 192 to 768, as said below
Outputs:
- attended: bfloat16 [24576, 4096], P(('group', 'dp'), 'tensor')
The draws below stay inside these ranges and needn't reach their ends.
Inputs may be any that keep to these rules, and one draw needn't show every extreme that they name: `prompt_len`: some sequence is full.
All inputs are finite; a program needn't handle non-finite values.
Results may differ from the reference program's by a relative error of at most 0.012.
The reference program's roundings to bfloat16 on the way (of `updated`, `normed` and `weights`) count: a program that leaves them out, or rounds other values in their place, can miss the bound.
Values may be sent and summed in bfloat16 or wider, within the bound.
No kernel may reach another device: no remote copies, remote signals or barrier semaphores. Data moves between devices by JAX's collectives and lax.ppermute only.
A program may use at most 64 MiB of HBM per device.

```python
import math
import jax
import jax.numpy as jnp
from jax import lax

D = 5120
HD = 128
HEAD_DEV = 2
SEQ = 768
HEADS = 32
KV_HEADS = 8
SEQS = 32
TOKENS = 24576


def draw_grad(key, part):
    key = jax.random.fold_in(key, 11)
    shape = (D, 2 * KV_HEADS, HEAD_DEV + 1, HD)
    rows = jnp.arange(D, dtype=jnp.float32) / (D - 1)
    ramp = (1.0 + 2.0 * rows)[:, None, None, None]
    slab_key = jax.random.fold_in(key, 5)
    block_key = jax.random.fold_in(key, 7)
    slab_factor = jnp.exp(jax.random.uniform(slab_key, (1, 2 * KV_HEADS, 1, 1), jnp.float32, -1.5, 1.5))
    block_table = jnp.exp(jax.random.uniform(block_key, (32,), jnp.float32, -1.5, 1.5))
    block_index = jnp.arange(D, dtype=jnp.int32) * 32 // D
    block_factor = jnp.take(block_table, block_index)[:, None, None, None]
    base = jnp.clip(jax.random.normal(key, shape, jnp.float32), -4.0, 4.0)
    values = 0.25 * base * ramp * slab_factor * block_factor
    return jnp.clip(values, -12.0, 12.0).astype(jnp.bfloat16)


def draw_prompt_len(key, part):
    key = jax.random.fold_in(key, 23)
    lengths = jax.random.randint(key, (SEQS,), SEQ // 4, SEQ + 1, dtype=jnp.int32)
    return lengths.at[0].set(SEQ)


def levels(stream_key, dims, pieces, smallest, top_value):
    level = 1.0
    for dim, parts in pieces:
        heights = jax.random.uniform(jax.random.fold_in(jax.random.fold_in(stream_key, 6), dim), (parts,), jnp.float32, smallest / len(pieces), top_value / len(pieces))
        level = level * jnp.repeat(jnp.exp(heights), dims[dim] // parts).reshape((-1,) + (1,) * (len(dims) - 1 - dim))
    return level


def normal_values(key, extent, scale, limit, cuts=(), kind=jnp.bfloat16):
    result = scale * jax.random.normal(key, extent, jnp.float32)
    if cuts:
        result = result * levels(key, extent, cuts, -0.22, 0.18)
    return jnp.clip(result, -limit, limit).astype(kind)


def setup_inputs(seed: int = 0) -> dict:
    seeds = jax.random.split(jax.random.key(seed), 10)
    activations = normal_values(seeds[0], (TOKENS, D), 1.0, 6.0, ((0, 32), (1, 16)))
    norm_gain = jnp.clip(jax.random.uniform(seeds[1], (D,), jnp.float32, 0.5, 1.5), 0.5, 1.5)
    master_weight = normal_values(seeds[2], (D, 2 * KV_HEADS, HEAD_DEV + 1, HD), D ** -0.5, 0.078125, ((0, 32), (1, 16)), jnp.float32)
    grad = draw_grad(jax.random.fold_in(seeds[9], 71), 0)
    moment = normal_values(seeds[4], (D, 2 * KV_HEADS, HEAD_DEV + 1, HD), ((D * 2 * KV_HEADS * (HEAD_DEV + 1) * HD) ** -0.5), 0.0024414062, ((0, 32), (1, 16)), jnp.float32)
    variance = jnp.clip(jnp.exp(math.log(6.357829107628277e-08) - 3.6888795 * jax.random.uniform(seeds[5], (D, 2 * KV_HEADS, HEAD_DEV + 1, HD), jnp.float32) ** levels(seeds[5], (D, 2 * KV_HEADS, HEAD_DEV + 1, HD), ((0, 32), (1, 16)), -0.2, 0.2)), 1.5894572324981482e-09, 6.357829107628277e-08)
    query_gain = jnp.clip(1.0 + 1.5 * jax.random.uniform(seeds[6], (HEADS, HD), jnp.float32) ** levels(seeds[6], (HEADS, HD), ((0, 16),), -0.2, 0.2), 1.0, 2.5)
    key_gain = jnp.clip(jax.random.uniform(seeds[7], (KV_HEADS, HD), jnp.float32, 1.0, 2.5), 1.0, 2.5)
    prompt_len = draw_prompt_len(jax.random.fold_in(seeds[9], 71), 0)
    return dict(activations=activations, norm_gain=norm_gain, master_weight=master_weight, grad=grad, moment=moment, variance=variance, query_gain=query_gain, key_gain=key_gain, prompt_len=prompt_len)


STEP_SCALE = 0.5
BETA_ONE = 0.9
BETA_TWO = 0.95
ROPE_BASE = 500000.0

def rope_tables(length, head_size):
    positions = jnp.arange(length, dtype=jnp.float32)
    exponent = jnp.arange(head_size // 2, dtype=jnp.float32) * 2.0 / head_size
    inverse = jnp.power(ROPE_BASE, -exponent)
    angles = positions[:, None] * inverse[None, :]
    return (jnp.cos(angles), jnp.sin(angles))

def rotate(inputs, cosine, sine):
    midpoint = inputs.shape[-1] // 2
    front_half = inputs[..., :midpoint]
    back_half = inputs[..., midpoint:]
    return jnp.concatenate([front_half * cosine - back_half * sine, back_half * cosine + front_half * sine], axis=-1)

def rms_scaled(inputs, gains):
    return inputs * lax.rsqrt(lax.optimization_barrier(jnp.mean(inputs * inputs, axis=-1, keepdims=True)) + 1e-06) * gains

def attend(query_proj, key_proj, value_proj, query_gain, key_gain, length):
    length_seq = query_proj.shape[0]
    head_count = query_proj.shape[1]
    pair_count = key_proj.shape[1]
    head_size = query_proj.shape[-1]
    cosine, sine = rope_tables(length_seq, head_size)
    cosine = cosine[:, None, :]
    sine = sine[:, None, :]
    queries = rms_scaled(query_proj, query_gain)
    keys_raw = rms_scaled(key_proj, key_gain)
    queries = (rotate(queries, cosine, sine) * head_size ** (-0.5)).astype(jnp.bfloat16)
    key_rot = rotate(keys_raw, cosine, sine).astype(jnp.bfloat16)
    value_rows = value_proj.astype(jnp.bfloat16)
    grouped = queries.reshape(length_seq, pair_count, head_count // pair_count, head_size)
    scores = jnp.einsum('qgje,kge->gjqk', grouped.astype(jnp.float32), key_rot.astype(jnp.float32))
    row_pos = jnp.arange(length_seq, dtype=jnp.int32)[:, None]
    col_pos = jnp.arange(length_seq, dtype=jnp.int32)[None, :]
    allowed = (col_pos <= row_pos) & (col_pos < length)
    scores = jnp.where(allowed[None, None], scores, -1e+30)
    highest = lax.optimization_barrier(jnp.max(scores, axis=-1, keepdims=True))
    weights = jnp.exp(scores - highest)
    weights = (weights / lax.optimization_barrier(jnp.sum(weights, axis=-1, keepdims=True))).astype(jnp.bfloat16)
    output = jnp.einsum('gjqk,kge->qgje', weights.astype(jnp.float32), value_rows.astype(jnp.float32))
    return output.astype(jnp.bfloat16).reshape(length_seq, -1)

def reference(activations, norm_gain, master_weight, grad, moment, variance, query_gain, key_gain, prompt_len):
    grad_full = grad.astype(jnp.float32)
    sumsq = jnp.sum(grad_full * grad_full)
    clip_factor = 1.0 / jnp.sqrt(sumsq + 1e-12)
    clipped = grad_full * clip_factor
    moment_new = BETA_ONE * moment + (1.0 - BETA_ONE) * clipped
    variance_new = BETA_TWO * variance + (1.0 - BETA_TWO) * clipped * clipped
    step_size = STEP_SCALE * D ** (-0.5)
    updated = (master_weight - step_size * moment_new / (jnp.sqrt(variance_new) + 1e-08)).astype(jnp.bfloat16)
    width_all = updated.shape[0]
    slab_count = updated.shape[1]
    head_dev = updated.shape[2] - 1
    head_size = updated.shape[3]
    query_weight = updated[:, :, :head_dev].reshape(width_all, slab_count * head_dev * head_size)
    pair_weight = updated[:, :, head_dev].reshape(width_all, slab_count * head_size)
    sequences = activations.reshape(-1, SEQ, width_all)

    def one_sequence(inputs):
        rows_in, length = inputs
        widened = rows_in.astype(jnp.float32)
        row_scale = lax.rsqrt(lax.optimization_barrier(jnp.mean(widened * widened, axis=-1, keepdims=True)) + 1e-06)
        normed = (widened * row_scale * norm_gain).astype(jnp.bfloat16)
        query_proj = jnp.dot(normed, query_weight, preferred_element_type=jnp.float32)
        query_proj = query_proj.reshape(SEQ, slab_count * head_dev, head_size)
        pair_proj = jnp.dot(normed, pair_weight, preferred_element_type=jnp.float32)
        pair_proj = pair_proj.reshape(SEQ, slab_count // 2, 2, head_size)
        return attend(query_proj, pair_proj[:, :, 0], pair_proj[:, :, 1], query_gain, key_gain, length)
    outputs = lax.map(one_sequence, (sequences, prompt_len))
    return outputs.reshape(-1, slab_count * head_dev * head_size)
```

```python
import jax
import jax.numpy as jnp
from jax import lax
from jax.sharding import Mesh, PartitionSpec as P

STEP_SCALE = 0.5
BETA_ONE = 0.9
BETA_TWO = 0.95
ROPE_BASE = 500000.0
AXES = ("xl", "core", "y", "z", "xh")
SIZES = (2, 2, 8, 8, 2)


def rope_tables(length, head_size):
    positions = jnp.arange(length, dtype=jnp.float32)
    exponent = jnp.arange(head_size // 2, dtype=jnp.float32) * 2.0 / head_size
    inverse = jnp.power(ROPE_BASE, -exponent)
    angles = positions[:, None] * inverse[None, :]
    return (jnp.cos(angles), jnp.sin(angles))


def rotate(inputs, cosine, sine):
    midpoint = inputs.shape[-1] // 2
    front_half = inputs[..., :midpoint]
    back_half = inputs[..., midpoint:]
    return jnp.concatenate(
        [front_half * cosine - back_half * sine, back_half * cosine + front_half * sine], axis=-1
    )


def rms_scaled(inputs, gains):
    return inputs * lax.rsqrt(jnp.mean(inputs * inputs, axis=-1, keepdims=True) + 1e-06) * gains


def swap(array, axis):
    return lax.ppermute(array, axis, [(0, 1), (1, 0)])


def global_sum(value):
    count = 1
    for size in SIZES:
        count *= size
    spread = jnp.broadcast_to(value, (count, 128))
    return jnp.sum(lax.all_to_all(spread, AXES, 0, 0, tiled=True)[:, 0])


def to_column(block, step):
    pairs = []
    for y in range(8):
        for slab in range(2):
            pairs.append((y * 2 + slab, (y + step + 2 * slab) % 8 * 2 + (y >> 1) % 2))
    return lax.ppermute(block, ("y", "xh"), pairs)


def shards(
    activations, norm_gain, master_weight, grad, moment, variance, query_gain, key_gain, prompt_len
):
    xl, y, z, xh = (lax.axis_index(a) for a in ("xl", "y", "z", "xh"))
    width_all = norm_gain.shape[0]
    seq_rows, width_part = activations.shape
    slab_rows, _, slab_heads, head_size = grad.shape
    head_dev = slab_heads - 1
    query_cols = head_dev * head_size
    slab_cols = slab_heads * head_size

    gathered = lax.all_gather(activations, "z", axis=1, tiled=True)

    grad_local = grad.astype(jnp.float32)
    sumsq = global_sum(jnp.sum(grad_local * grad_local))
    clip_factor = 1.0 / jnp.sqrt(sumsq + 1e-12)
    clipped = grad_local * clip_factor
    moment_new = BETA_ONE * moment + (1.0 - BETA_ONE) * clipped
    variance_new = BETA_TWO * variance + (1.0 - BETA_TWO) * clipped * clipped
    step_size = STEP_SCALE * width_all ** (-0.5)
    updated = (master_weight - step_size * moment_new / (jnp.sqrt(variance_new) + 1e-08)).astype(
        jnp.bfloat16
    )
    updated = updated.reshape(slab_rows, slab_cols)

    arrived = jnp.stack([to_column(updated, step) for step in range(8)])
    rows = []
    for high in range(2):
        for low in range(2):
            source = high * 4 + xh * 2 + low
            left = lax.dynamic_index_in_dim(arrived, (y - source) & 7, 0, False)
            right = lax.dynamic_index_in_dim(arrived, (y - source - 2) & 7, 0, False)
            rows.append(jnp.concatenate([left, right], axis=1))
    own_rows = jnp.concatenate(rows, axis=0)
    other_rows = swap(own_rows, "xl")
    own_weight = lax.all_gather(own_rows, "core", axis=0, tiled=True)
    other_weight = lax.all_gather(other_rows, "core", axis=0, tiled=True)

    widened = gathered.astype(jnp.float32)
    square = jnp.sum(widened * widened, axis=-1)
    square = square + swap(square, "xh")
    row_scale = lax.rsqrt(square / width_all + 1e-06)
    gain = lax.dynamic_index_in_dim(norm_gain.reshape(8, 2, width_part), xh, 1, False).reshape(-1)
    normed = (widened * row_scale[:, None] * gain).astype(jnp.bfloat16)
    half = normed.shape[1] // 2
    own_normed = lax.dynamic_slice_in_dim(normed, xl * half, half, 1)
    other_normed = lax.dynamic_slice_in_dim(normed, (1 - xl) * half, half, 1)
    partial = jnp.dot(own_normed, own_weight, preferred_element_type=jnp.float32)
    partial += jnp.dot(other_normed, other_weight, preferred_element_type=jnp.float32)

    def picked(slab):
        queries = lax.dynamic_slice_in_dim(partial, slab * slab_cols, query_cols, 1)
        return jnp.concatenate([queries, partial[:, query_cols:slab_cols], partial[:, slab_cols + query_cols :]], axis=1)

    projected = picked(xh) + swap(picked(1 - xh).astype(jnp.bfloat16), "xh").astype(jnp.float32)

    cosine, sine = rope_tables(seq_rows, head_size)
    gain_row = lax.dynamic_slice_in_dim(key_gain, z, 1, 0)[0]
    query_proj = projected[:, :query_cols].reshape(seq_rows, head_dev, head_size)
    queries = rms_scaled(query_proj, query_gain)
    queries = (rotate(queries, cosine[:, None, :], sine[:, None, :]) * head_size ** (-0.5)).astype(
        jnp.bfloat16
    )
    key_rot = rotate(
        rms_scaled(projected[:, query_cols : query_cols + head_size], gain_row), cosine, sine
    ).astype(jnp.bfloat16)
    value_rows = projected[:, query_cols + head_size :].astype(jnp.bfloat16)
    scores = jnp.einsum("qhe,ke->hqk", queries, key_rot, preferred_element_type=jnp.float32)
    row_pos = jnp.arange(seq_rows, dtype=jnp.int32)[:, None]
    col_pos = jnp.arange(seq_rows, dtype=jnp.int32)[None, :]
    allowed = (col_pos <= row_pos) & (col_pos < prompt_len[0])
    scores = jnp.where(allowed[None], scores, -1e30)
    highest = jnp.max(scores, axis=-1, keepdims=True)
    weights = jnp.exp(scores - highest)
    weights = (weights / jnp.sum(weights, axis=-1, keepdims=True)).astype(jnp.bfloat16)
    output = jnp.einsum("hqk,ke->qhe", weights, value_rows, preferred_element_type=jnp.float32)
    return output.astype(jnp.bfloat16).reshape(seq_rows, query_cols)


def solution(mesh):
    fine = Mesh(mesh.devices.reshape(SIZES), AXES)
    rows, cols = ("xl", "core", "y"), ("z", "xh")
    slab = P(rows, cols, None, None)
    in_specs = (P(rows, cols), P(), slab, slab, slab, slab, P(cols, None), P(), P(rows))
    return jax.shard_map(
        shards, mesh=fine, in_specs=in_specs, out_specs=P(rows, cols), check_vma=False
    )
```

```python
import functools

import jax
import jax.numpy as jnp
import numpy as np
from jax import lax
from jax.experimental import pallas as pl
from jax.experimental.pallas import tpu as pltpu
from jax.sharding import Mesh, PartitionSpec as P

STEP_SCALE = 0.5
BETA_ONE = 0.9
BETA_TWO = 0.95
ROPE_BASE = 500000.0
AXES = ("xl", "core", "y", "z", "xh")
SIZES = (2, 2, 8, 8, 2)


def rope_tables(length, head_size):
    exponent = np.arange(head_size // 2, dtype=np.float32) * np.float32(2.0) / head_size
    inverse = np.power(np.float64(ROPE_BASE), -exponent.astype(np.float64)).astype(np.float32)
    angles = np.arange(length, dtype=np.float32)[:, None] * inverse[None, :]
    cosine = np.cos(angles.astype(np.float64)).astype(np.float32)
    sine = np.sin(angles.astype(np.float64)).astype(np.float32)
    return np.concatenate([cosine, cosine], axis=1), np.concatenate([-sine, sine], axis=1)


def rms_rotated(inputs, gain, cosine, sine):
    scale = lax.rsqrt(jnp.mean(inputs * inputs, axis=-1, keepdims=True) + 1e-06)
    scaled = inputs * scale * gain
    return scaled * cosine + pltpu.roll(scaled, scaled.shape[-1] // 2, 1) * sine


def assemble_kernel(place_ref, *refs):
    *blocks, out_ref = refs
    rows, cols = blocks[0].shape[1:]
    half = out_ref.shape[0] // 2
    for step, block in enumerate(blocks):
        row = pl.multiple_of(place_ref[0, step] * rows, 32)
        col = pl.multiple_of(place_ref[1, step] * cols, 128)
        for near in range(2):
            out_ref[pl.ds(near * half + row, rows), pl.ds(col, cols)] = block[near]


def assemble(place, blocks):
    rows, cols = blocks[0].shape[1:]
    vmem = pl.BlockSpec(memory_space=pltpu.VMEM)
    return pl.pallas_call(
        assemble_kernel,
        out_shape=jax.ShapeDtypeStruct((len(blocks) * rows, 2 * cols), blocks[0].dtype),
        in_specs=[pl.BlockSpec(memory_space=pltpu.SMEM)] + [vmem] * len(blocks),
        out_specs=vmem,
        compiler_params=pltpu.CompilerParams(vmem_limit_bytes=24 << 20),
        name="assemble",
    )(place, *blocks)


def attend_kernel(tile, limit_ref, own_ref, got_ref, query_gain_ref, key_gain_ref, cos_ref, sin_ref, out_ref):
    length, head = cos_ref.shape
    heads = query_gain_ref.shape[0]
    wide = heads * head
    limit = limit_ref[0]

    def summed(start, rows, col):
        got = got_ref[start : start + rows, col : col + head].astype(jnp.float32)
        return own_ref[start : start + rows, col : col + head] + got

    key_gain = key_gain_ref[...]
    keys = rms_rotated(summed(0, length, wide), key_gain, cos_ref[...], sin_ref[...])
    keys = keys.astype(jnp.bfloat16)
    values = summed(0, length, wide + head).astype(jnp.bfloat16)
    for start in range(0, length, tile):
        seen = start + tile
        row = start + lax.broadcasted_iota(jnp.int32, (tile, seen), 0)
        col = lax.broadcasted_iota(jnp.int32, (tile, seen), 1)
        allowed = (col <= row) & (col < limit)
        cosine, sine = cos_ref[start:seen, :], sin_ref[start:seen, :]
        for j in range(heads):
            query = rms_rotated(summed(start, tile, j * head), query_gain_ref[j : j + 1, :], cosine, sine)
            query = (query * head**-0.5).astype(jnp.bfloat16)
            scores = lax.dot_general(
                query, keys[:seen], (((1,), (1,)), ((), ())), preferred_element_type=jnp.float32
            )
            scores = jnp.where(allowed, scores, -1e30)
            weights = jnp.exp(scores - jnp.max(scores, axis=-1, keepdims=True))
            weights = weights / jnp.sum(weights, axis=-1, keepdims=True)
            output = jnp.dot(weights.astype(jnp.bfloat16), values[:seen], preferred_element_type=jnp.float32)
            out_ref[start:seen, j * head : (j + 1) * head] = output.astype(out_ref.dtype)


def attend(limit, own, got, query_gain, key_gain):
    length = own.shape[0]
    heads, head = query_gain.shape
    cosine, sine = rope_tables(length, head)
    vmem = pl.BlockSpec(memory_space=pltpu.VMEM)
    return pl.pallas_call(
        functools.partial(attend_kernel, 256),
        out_shape=jax.ShapeDtypeStruct((length, heads * head), jnp.bfloat16),
        in_specs=[pl.BlockSpec(memory_space=pltpu.SMEM)] + [vmem] * 6,
        out_specs=vmem,
        compiler_params=pltpu.CompilerParams(vmem_limit_bytes=40 << 20),
        name="attend",
    )(limit, own, got, query_gain, key_gain, cosine, sine)


def swap(array, axis):
    return lax.ppermute(array, axis, [(0, 1), (1, 0)])


def global_sum(value):
    count = 1
    for size in SIZES:
        count *= size
    spread = jnp.broadcast_to(value, (count, 128))
    return jnp.sum(lax.all_to_all(spread, AXES, 0, 0, tiled=True)[:, 0])


def to_column(block, other):
    pairs = []
    for xl in range(2):
        for y in range(8):
            for slab in range(2):
                target = ((xl ^ other) * 8 + (y + 2 * slab) % 8) * 2 + (y >> 1) % 2
                pairs.append(((xl * 8 + y) * 2 + slab, target))
    return lax.ppermute(block, ("xl", "y", "xh"), pairs)


def along(array, axis, step):
    size = lax.axis_size(axis)
    return lax.ppermute(array, axis, [(i, (i + step) % size) for i in range(size)])


def shards(
    activations, norm_gain, master_weight, grad, moment, variance, query_gain, key_gain, prompt_len
):
    xl, core, y, z, xh = (lax.axis_index(a) for a in AXES)
    width_all = norm_gain.shape[0]
    seq_rows, width_part = activations.shape
    slab_rows, _, slab_heads, head_size = grad.shape
    head_dev = slab_heads - 1
    query_cols = head_dev * head_size
    slab_cols = slab_heads * head_size

    gathered = lax.all_gather(activations, "z", axis=1, tiled=True)

    grad_local = grad.astype(jnp.float32)
    sumsq = global_sum(jnp.sum(grad_local * grad_local))
    clip_factor = 1.0 / jnp.sqrt(sumsq + 1e-12)
    clipped = grad_local * clip_factor
    moment_new = BETA_ONE * moment + (1.0 - BETA_ONE) * clipped
    variance_new = BETA_TWO * variance + (1.0 - BETA_TWO) * clipped * clipped
    step_size = STEP_SCALE * width_all ** (-0.5)
    updated = (master_weight - step_size * moment_new / (jnp.sqrt(variance_new) + 1e-08)).astype(
        jnp.bfloat16
    )
    updated = updated.reshape(slab_rows, slab_cols)

    home = jnp.stack([to_column(updated, 0), to_column(updated, 1)])
    arrived = {0: home}
    up = down = home
    up = arrived[1] = along(up, "y", 1)
    down = arrived[7] = along(down, "y", -1)
    up = arrived[2] = along(up, "y", 1)
    down = arrived[6] = along(down, "y", -1)
    gathered, up, down = lax.optimization_barrier((gathered, up, down))

    widened = gathered.astype(jnp.float32)
    square = jnp.sum(widened * widened, axis=-1)
    square = square + swap(square, "xh")
    row_scale = lax.rsqrt(square / width_all + 1e-06)
    gain = lax.dynamic_index_in_dim(norm_gain.reshape(8, 2, width_part), xh, 1, False).reshape(-1)
    normed = (widened * row_scale[:, None] * gain).astype(jnp.bfloat16)

    up = arrived[3] = along(up, "y", 1)
    down = arrived[5] = along(down, "y", -1)
    normed, up = lax.optimization_barrier((normed, up))
    arrived[4] = along(up, "y", 1)

    source = (y - jnp.arange(8)) & 7
    native = ((source >> 1) & 1) == xh
    shifted = (source - 2) & 7
    origin = jnp.where(native, source, shifted)
    place = jnp.stack([(origin >> 2) * 2 + (origin & 1), jnp.where(native, 0, 1)]).astype(jnp.int32)
    own_weight = assemble(place, [arrived[step] for step in range(8)])
    other_weight = swap(own_weight, "core")

    quarter = normed.shape[1] // 4

    def matching(lane):
        near = lax.dynamic_slice_in_dim(normed, (xl * 2 + lane) * quarter, quarter, 1)
        far = lax.dynamic_slice_in_dim(normed, (2 - xl * 2 + lane) * quarter, quarter, 1)
        return jnp.concatenate([near, far], axis=1)

    partial = jnp.dot(matching(core), own_weight, preferred_element_type=jnp.float32)
    partial += jnp.dot(matching(1 - core), other_weight, preferred_element_type=jnp.float32)

    def picked(slab):
        queries = lax.dynamic_slice_in_dim(partial, slab * slab_cols, query_cols, 1)
        return jnp.concatenate([queries, partial[:, query_cols:slab_cols], partial[:, slab_cols + query_cols :]], axis=1)

    got = swap(picked(1 - xh).astype(jnp.bfloat16), "xh")
    gain_row = lax.dynamic_slice_in_dim(key_gain, z, 1, 0)
    return attend(prompt_len, picked(xh), got, query_gain, gain_row)


def solution(mesh):
    fine = Mesh(mesh.devices.reshape(SIZES), AXES)
    rows, cols = ("xl", "core", "y"), ("z", "xh")
    slab = P(rows, cols, None, None)
    in_specs = (P(rows, cols), P(), slab, slab, slab, slab, P(cols, None), P(), P(rows))
    return jax.shard_map(
        shards, mesh=fine, in_specs=in_specs, out_specs=P(rows, cols), check_vma=False
    )
```

```python
import functools

import jax
import jax.numpy as jnp
import numpy as np
from jax import lax
from jax.experimental import pallas as pl
from jax.experimental.pallas import tpu as pltpu
from jax.sharding import Mesh, PartitionSpec as P

STEP_SCALE = 0.5
BETA_ONE = 0.9
BETA_TWO = 0.95
ROPE_BASE = 500000.0
AXES = ("xl", "core", "y", "z", "xh")
SIZES = (2, 2, 8, 8, 2)


def rope_tables(length, head_size):
    exponent = np.arange(head_size // 2, dtype=np.float32) * np.float32(2.0) / head_size
    inverse = np.power(np.float64(ROPE_BASE), -exponent.astype(np.float64)).astype(np.float32)
    angles = np.arange(length, dtype=np.float32)[:, None] * inverse[None, :]
    cosine = np.cos(angles.astype(np.float64)).astype(np.float32)
    sine = np.sin(angles.astype(np.float64)).astype(np.float32)
    return np.concatenate([cosine, cosine], axis=1), np.concatenate([-sine, sine], axis=1)


def rms_rotated(inputs, gain, cosine, sine):
    scale = lax.rsqrt(jnp.mean(inputs * inputs, axis=-1, keepdims=True) + 1e-06)
    scaled = inputs * scale * gain
    return scaled * cosine + pltpu.roll(scaled, scaled.shape[-1] // 2, 1) * sine


VMEM = pl.BlockSpec(memory_space=pltpu.VMEM)
SMEM = pl.BlockSpec(memory_space=pltpu.SMEM)


def local_call(kernel, name, out_shape, in_specs, out_specs):
    params = pltpu.CompilerParams(vmem_limit_bytes=40 << 20)
    return pl.pallas_call(
        kernel, out_shape=out_shape, in_specs=in_specs, out_specs=out_specs, compiler_params=params, name=name
    )


def assemble_kernel(place_ref, *refs):
    *blocks, out_ref = refs
    rows, cols = blocks[0].shape[1:]
    half = out_ref.shape[0] // 2
    head = out_ref.shape[1] // 6
    wide = cols - head
    for step, block in enumerate(blocks):
        row = pl.multiple_of(place_ref[0, step] * rows, 32)
        query_col = pl.multiple_of(place_ref[1, step] * wide, 128)
        pair_col = pl.multiple_of(2 * wide + place_ref[2, step] * head, 128)
        for near in range(2):
            span = pl.ds(near * half + row, rows)
            out_ref[span, pl.ds(query_col, wide)] = block[near, :, :wide]
            out_ref[span, pl.ds(pair_col, head)] = block[near, :, wide:]


def assemble(place, blocks):
    rows, cols = blocks[0].shape[1:]
    shape = jax.ShapeDtypeStruct((len(blocks) * rows, 2 * cols), blocks[0].dtype)
    call = local_call(assemble_kernel, "assemble", shape, [SMEM] + [VMEM] * len(blocks), VMEM)
    return call(place, *blocks)


def squares_kernel(*refs):
    *blocks, out_ref = refs
    total = None
    for block in blocks:
        wide = block[...].astype(jnp.float32)
        square = jnp.sum(wide * wide, axis=0, keepdims=True)
        total = square if total is None else total + square
    out_ref[...] = total


def squares(blocks):
    shape = jax.ShapeDtypeStruct((1, blocks[0].shape[1]), jnp.float32)
    return local_call(squares_kernel, "squares", shape, [VMEM] * len(blocks), VMEM)(*blocks)


def normalise_kernel(width_all, place_ref, square_ref, other_ref, gain_ref, *refs):
    *blocks, out_ref = refs
    rows = blocks[0].shape[0]
    scale = lax.rsqrt((square_ref[...] + other_ref[...]) / width_all + 1e-06)
    for step, block in enumerate(blocks):
        row = pl.multiple_of(place_ref[step] * rows, 64)
        gain = gain_ref[step * rows : (step + 1) * rows, :]
        out_ref[pl.ds(row, rows), :] = (block[...].astype(jnp.float32) * scale * gain).astype(out_ref.dtype)


def normalise(width_all, place, square, other, gain, blocks):
    rows, cols = blocks[0].shape
    shape = jax.ShapeDtypeStruct((len(blocks) * rows, cols), jnp.bfloat16)
    kernel = functools.partial(normalise_kernel, width_all)
    call = local_call(kernel, "normalise", shape, [SMEM] + [VMEM] * (3 + len(blocks)), VMEM)
    return call(place, square, other, gain, *blocks)


def attend_kernel(tile, first, length, limit_ref, own_ref, got_ref, query_gain_ref, key_gain_ref, cos_ref, sin_ref, *refs):
    before, out_ref, keys_ref, values_ref = refs[:-3], *refs[-3:]
    heads, head = query_gain_ref.shape
    wide = heads * head
    limit = limit_ref[0]
    rows = own_ref.shape[0]
    if before:
        out_ref[:first, :] = before[0][...]
        keys_ref[:first, :] = before[1][...]
        values_ref[:first, :] = before[2][...]

    def summed(start, size, own_col, got_col):
        got = got_ref[start : start + size, got_col : got_col + head].astype(jnp.float32)
        return own_ref[start : start + size, own_col : own_col + head] + got

    cosine, sine = cos_ref[...], sin_ref[...]
    keys = rms_rotated(summed(0, rows, 2 * wide, wide), key_gain_ref[...], cosine, sine)
    keys_ref[first:, :] = keys.astype(jnp.bfloat16)
    values_ref[first:, :] = summed(0, rows, 2 * wide + head, wide + head).astype(jnp.bfloat16)
    for start in range(0, rows, tile):
        seen = first + start + tile
        row = first + start + lax.broadcasted_iota(jnp.int32, (tile, seen), 0)
        col = lax.broadcasted_iota(jnp.int32, (tile, seen), 1)
        allowed = (col <= row) & (col < limit)
        cosine, sine = cos_ref[start : start + tile, :], sin_ref[start : start + tile, :]
        for j in range(heads):
            projected = summed(start, tile, j * head, j * head)
            query = rms_rotated(projected, query_gain_ref[j : j + 1, :], cosine, sine)
            query = (query * head**-0.5).astype(jnp.bfloat16)
            scores = lax.dot_general(
                query, keys_ref[:seen, :], (((1,), (1,)), ((), ())), preferred_element_type=jnp.float32
            )
            scores = jnp.where(allowed, scores, -1e30)
            weights = jnp.exp(scores - jnp.max(scores, axis=-1, keepdims=True))
            weights = weights / jnp.sum(weights, axis=-1, keepdims=True)
            output = jnp.dot(weights.astype(jnp.bfloat16), values_ref[:seen, :], preferred_element_type=jnp.float32)
            out_ref[first + start : seen, j * head : (j + 1) * head] = output.astype(out_ref.dtype)


def attend(limit, own, got, query_gain, key_gain, tables, before):
    rows = own.shape[0]
    heads, head = query_gain.shape
    first = before[0].shape[0] if before else 0
    cosine, sine = (table[first : first + rows] for table in tables)
    shape = [jax.ShapeDtypeStruct((first + rows, n), jnp.bfloat16) for n in (heads * head, head, head)]
    kernel = functools.partial(attend_kernel, rows // 2, first, first + rows)
    call = local_call(kernel, "attend", shape, [SMEM] + [VMEM] * (6 + len(before)), [VMEM] * 3)
    return call(limit, own, got, query_gain, key_gain, cosine, sine, *before)


def swap(array, axis):
    return lax.ppermute(array, axis, [(0, 1), (1, 0)])


def global_sum(value):
    count = 1
    for size in SIZES:
        count *= size
    spread = jnp.broadcast_to(value, (count, 128))
    return jnp.sum(lax.all_to_all(spread, AXES, 0, 0, tiled=True)[:, 0])


def to_column(block, other):
    pairs = []
    for xl in range(2):
        for y in range(8):
            for slab in range(2):
                target = ((xl ^ other) * 8 + (y + 2 * slab) % 8) * 2 + (y >> 1) % 2
                pairs.append(((xl * 8 + y) * 2 + slab, target))
    return lax.ppermute(block, ("xl", "y", "xh"), pairs)


def along(array, axis, step):
    size = lax.axis_size(axis)
    return lax.ppermute(array, axis, [(i, (i + step) % size) for i in range(size)])


def shards(
    activations, norm_gain, master_weight, grad, moment, variance, query_gain, key_gain, prompt_len
):
    xl, core, y, z, xh = (lax.axis_index(a) for a in AXES)
    width_all = norm_gain.shape[0]
    seq_rows, width_part = activations.shape
    slab_rows, _, slab_heads, head_size = grad.shape
    steps = jnp.arange(8)

    features = {0: activations.T}
    features[1] = along(features[0], "z", 1)
    features[7] = along(features[0], "z", -1)

    grad_local = grad.astype(jnp.float32)
    sumsq = global_sum(jnp.sum(grad_local * grad_local))
    sumsq, features[1], features[7] = lax.optimization_barrier((sumsq, features[1], features[7]))
    clip_factor = 1.0 / jnp.sqrt(sumsq + 1e-12)
    clipped = grad_local * clip_factor
    moment_new = BETA_ONE * moment + (1.0 - BETA_ONE) * clipped
    variance_new = BETA_TWO * variance + (1.0 - BETA_TWO) * clipped * clipped
    step_size = STEP_SCALE * width_all ** (-0.5)
    updated = (master_weight - step_size * moment_new / (jnp.sqrt(variance_new) + 1e-08)).astype(
        jnp.bfloat16
    )
    updated = updated.reshape(slab_rows, slab_heads * head_size)

    home = jnp.stack([to_column(updated, 0), to_column(updated, 1)])
    features[2] = along(features[1], "z", 1)
    features[6] = along(features[7], "z", -1)
    home, features[2], features[6] = lax.optimization_barrier((home, features[2], features[6]))

    arrived = {0: home}
    arrived[1] = along(home, "y", 1)
    arrived[7] = along(home, "y", -1)
    features[3] = along(features[2], "z", 1)
    features[5] = along(features[6], "z", -1)
    arrived[1], arrived[7], features[3] = lax.optimization_barrier((arrived[1], arrived[7], features[3]))

    arrived[2] = along(arrived[1], "y", 1)
    arrived[6] = along(arrived[7], "y", -1)
    features[4] = along(features[3], "z", 1)
    arrived[2], arrived[6], features[4], features[5] = lax.optimization_barrier(
        (arrived[2], arrived[6], features[4], features[5])
    )

    arrived[3] = along(arrived[2], "y", 1)
    arrived[5] = along(arrived[6], "y", -1)
    blocks = [features[step] for step in range(8)]
    square = squares(blocks)
    arrived[3], square = lax.optimization_barrier((arrived[3], square))
    arrived[4] = along(arrived[3], "y", 1)

    other_square = swap(square, "xh")
    origin = (z - steps) & 7
    gain = norm_gain.reshape(8, 2, width_part)[origin, xh].reshape(-1, 1)
    place = ((((origin >> 1) & 1) ^ core) * 2 + ((origin >> 2) ^ xl)) * 2 + (origin & 1)
    normed = normalise(float(width_all), place.astype(jnp.int32), square, other_square, gain, blocks)

    source = (y - steps) & 7
    native = ((source >> 1) & 1) == xh
    origin = jnp.where(native, source, (source - 2) & 7)
    slab = jnp.where(native, 0, 1)
    place = jnp.stack([(origin >> 2) * 2 + (origin & 1), slab ^ xh, slab]).astype(jnp.int32)
    own_weight = assemble(place, [arrived[step] for step in range(8)])
    other_weight = swap(own_weight, "core")

    tables = rope_tables(seq_rows, head_size)
    gain_row = lax.dynamic_slice_in_dim(key_gain, z, 1, 0)
    half = normed.shape[0] // 2
    query_cols = (slab_heads - 1) * head_size
    part = seq_rows // 2

    def product(rows, weight):
        return lax.dot_general(rows, weight, (((0,), (0,)), ((), ())), preferred_element_type=jnp.float32)

    result = ()
    for start in range(0, seq_rows, part):
        tokens = normed[:, start : start + part]
        partial = product(tokens[:half], own_weight) + product(tokens[half:], other_weight)
        got = swap(partial[:, query_cols:].astype(jnp.bfloat16), "xh")
        result = attend(prompt_len, partial, got, query_gain, gain_row, tables, tuple(result))
    return result[0]


def solution(mesh):
    fine = Mesh(mesh.devices.reshape(SIZES), AXES)
    rows, cols = ("xl", "core", "y"), ("z", "xh")
    slab = P(rows, cols, None, None)
    in_specs = (P(rows, cols), P(), slab, slab, slab, slab, P(cols, None), P(), P(rows))
    return jax.shard_map(
        shards, mesh=fine, in_specs=in_specs, out_specs=P(rows, cols), check_vma=False
    )
```

```python
import functools

import jax
import jax.numpy as jnp
import numpy as np
from jax import lax
from jax.experimental import pallas as pl
from jax.experimental.pallas import tpu as pltpu
from jax.sharding import Mesh, PartitionSpec as P

STEP_SCALE = 0.5
BETA_ONE = 0.9
BETA_TWO = 0.95
ROPE_BASE = 500000.0
AXES = ("xl", "core", "y", "z", "xh")
SIZES = (2, 2, 8, 8, 2)


def rope_tables(length, head_size):
    exponent = np.arange(head_size // 2, dtype=np.float32) * np.float32(2.0) / head_size
    inverse = np.power(np.float64(ROPE_BASE), -exponent.astype(np.float64)).astype(np.float32)
    angles = np.arange(length, dtype=np.float32)[:, None] * inverse[None, :]
    cosine = np.cos(angles.astype(np.float64)).astype(np.float32)
    sine = np.sin(angles.astype(np.float64)).astype(np.float32)
    return np.concatenate([cosine, cosine], axis=1), np.concatenate([-sine, sine], axis=1)


def rms_rotated(inputs, gain, cosine, sine):
    scale = lax.rsqrt(jnp.mean(inputs * inputs, axis=-1, keepdims=True) + 1e-06)
    scaled = inputs * scale * gain
    return scaled * cosine + pltpu.roll(scaled, scaled.shape[-1] // 2, 1) * sine


VMEM = pl.BlockSpec(memory_space=pltpu.VMEM)
SMEM = pl.BlockSpec(memory_space=pltpu.SMEM)


def local_call(kernel, name, out_shape, in_specs, out_specs):
    params = pltpu.CompilerParams(vmem_limit_bytes=8 << 20)
    return pl.pallas_call(
        kernel, out_shape=out_shape, in_specs=in_specs, out_specs=out_specs, compiler_params=params, name=name
    )


def assemble_kernel(place_ref, home_ref, *refs):
    *step_refs, last_ref, early_ref, late_ref, out_ref = refs
    _, _, rows, cols = home_ref.shape
    head = out_ref.shape[1] // 6
    wide = cols - head

    def put(step, lane, block_ref, *index):
        row = pl.multiple_of(place_ref[0, step] * rows, 32)
        query_col = pl.multiple_of(place_ref[1, step] * wide, 128)
        pair_col = pl.multiple_of(2 * wide + place_ref[2, step] * head, 128)
        for near in range(2):
            span = pl.ds((lane * 2 + near) * 4 * rows + row, rows)
            out_ref[span, pl.ds(query_col, wide)] = block_ref[*index, near, :, :wide]
            out_ref[span, pl.ds(pair_col, head)] = block_ref[*index, near, :, wide:]

    for lane in range(2):
        put(0, lane, home_ref, lane)
        for step in range(3):
            put(1 + step, lane, step_refs[step], lane)
        for step in range(2):
            put(5 + step, 1 - lane, early_ref, step, lane)
        put(7, 1 - lane, late_ref, lane)
    put(4, 0, last_ref)
    put(4, 1, late_ref, 2)


def assemble(place, home, *rest):
    _, _, rows, cols = home.shape
    shape = jax.ShapeDtypeStruct((16 * rows, 2 * cols), home.dtype)
    call = local_call(assemble_kernel, "assemble", shape, [SMEM] + [VMEM] * (1 + len(rest)), VMEM)
    return call(place, home, *rest)


def squares_kernel(parts, features_ref, out_ref):
    rows = features_ref.shape[0] // parts
    total = None
    for step in range(parts):
        wide = features_ref[step * rows : (step + 1) * rows, :].astype(jnp.float32)
        square = jnp.sum(wide * wide, axis=0, keepdims=True)
        total = square if total is None else total + square
    out_ref[...] = total


def squares(parts, features):
    shape = jax.ShapeDtypeStruct((1, features.shape[1]), jnp.float32)
    return local_call(functools.partial(squares_kernel, parts), "squares", shape, [VMEM], VMEM)(features)


def normalise_kernel(width_all, parts, place_ref, square_ref, other_ref, gain_ref, features_ref, out_ref):
    rows = features_ref.shape[0] // parts
    scale = lax.rsqrt((square_ref[...] + other_ref[...]) / width_all + 1e-06)
    for step in range(parts):
        span = slice(step * rows, (step + 1) * rows)
        row = pl.multiple_of(place_ref[step] * rows, 64)
        scaled = features_ref[span, :].astype(jnp.float32) * scale * gain_ref[span, :]
        out_ref[pl.ds(row, rows), :] = scaled.astype(out_ref.dtype)


def normalise(width_all, parts, place, square, other, gain, features):
    shape = jax.ShapeDtypeStruct(features.shape, jnp.bfloat16)
    kernel = functools.partial(normalise_kernel, width_all, parts)
    call = local_call(kernel, "normalise", shape, [SMEM] + [VMEM] * 4, VMEM)
    return call(place, square, other, gain, features)


def attend_kernel(tile, first, length, limit_ref, own_ref, got_ref, query_gain_ref, key_gain_ref, cos_ref, sin_ref, *refs):
    before, out_ref, keys_ref, values_ref = refs[:-3], *refs[-3:]
    heads, head = query_gain_ref.shape
    wide = heads * head
    limit = limit_ref[0]
    rows = own_ref.shape[0]
    if before:
        out_ref[:first, :] = before[0][...]
        keys_ref[:first, :] = before[1][...]
        values_ref[:first, :] = before[2][...]

    def summed(start, size, own_col, got_col):
        got = got_ref[start : start + size, got_col : got_col + head].astype(jnp.float32)
        return own_ref[start : start + size, own_col : own_col + head] + got

    cosine, sine = cos_ref[...], sin_ref[...]
    keys = rms_rotated(summed(0, rows, 2 * wide, wide), key_gain_ref[...], cosine, sine)
    keys_ref[first:, :] = keys.astype(jnp.bfloat16)
    values_ref[first:, :] = summed(0, rows, 2 * wide + head, wide + head).astype(jnp.bfloat16)
    for start in range(0, rows, tile):
        seen = first + start + tile
        row = first + start + lax.broadcasted_iota(jnp.int32, (tile, seen), 0)
        col = lax.broadcasted_iota(jnp.int32, (tile, seen), 1)
        allowed = (col <= row) & (col < limit)
        cosine, sine = cos_ref[start : start + tile, :], sin_ref[start : start + tile, :]
        for j in range(heads):
            projected = summed(start, tile, j * head, j * head)
            query = rms_rotated(projected, query_gain_ref[j : j + 1, :], cosine, sine)
            query = (query * head**-0.5).astype(jnp.bfloat16)
            scores = lax.dot_general(
                query, keys_ref[:seen, :], (((1,), (1,)), ((), ())), preferred_element_type=jnp.float32
            )
            scores = jnp.where(allowed, scores, -1e30)
            weights = jnp.exp(scores - jnp.max(scores, axis=-1, keepdims=True))
            weights = weights / jnp.sum(weights, axis=-1, keepdims=True)
            output = jnp.dot(weights.astype(jnp.bfloat16), values_ref[:seen, :], preferred_element_type=jnp.float32)
            out_ref[first + start : seen, j * head : (j + 1) * head] = output.astype(out_ref.dtype)


def attend(limit, own, got, query_gain, key_gain, tables, before):
    rows = own.shape[0]
    heads, head = query_gain.shape
    first = before[0].shape[0] if before else 0
    cosine, sine = (table[first : first + rows] for table in tables)
    shape = [jax.ShapeDtypeStruct((first + rows, n), jnp.bfloat16) for n in (heads * head, head, head)]
    kernel = functools.partial(attend_kernel, rows // 2, first, first + rows)
    call = local_call(kernel, "attend", shape, [SMEM] + [VMEM] * (6 + len(before)), [VMEM] * 3)
    return call(limit, own, got, query_gain, key_gain, cosine, sine, *before)


def swap(array, axis):
    return lax.ppermute(array, axis, [(0, 1), (1, 0)])


def global_sum(value):
    count = 1
    for size in SIZES:
        count *= size
    spread = jnp.broadcast_to(value, (count, 128))
    return jnp.sum(lax.all_to_all(spread, AXES, 0, 0, tiled=True)[:, 0])


def to_column(block, other):
    pairs = []
    for xl in range(2):
        for y in range(8):
            for slab in range(2):
                column = (y >> 1) % 2
                target = y if slab == column else (y + (1 if y % 2 else -1)) % 8
                pairs.append(((xl * 8 + y) * 2 + slab, ((xl ^ other) * 8 + target) * 2 + column))
    return lax.ppermute(block, ("xl", "y", "xh"), pairs)


def onward(block):
    pairs = [(y, (y + 1) % 8) for y in range(8)] + [(8 + y, 8 + (y - 1) % 8) for y in range(8)]
    return lax.ppermute(block, ("core", "y"), pairs)


def shards(
    activations, norm_gain, master_weight, grad, moment, variance, query_gain, key_gain, prompt_len
):
    xl, core, y, z, xh = (lax.axis_index(a) for a in AXES)
    width_all = norm_gain.shape[0]
    seq_rows, width_part = activations.shape
    slab_rows, _, slab_heads, head_size = grad.shape
    steps = jnp.arange(8)

    gathered = lax.all_gather(activations.T, "z", axis=0, tiled=True)

    grad_local = grad.astype(jnp.float32)
    sumsq = global_sum(jnp.sum(grad_local * grad_local))
    clip_factor = 1.0 / jnp.sqrt(sumsq + 1e-12)
    clipped = grad_local * clip_factor
    moment_new = BETA_ONE * moment + (1.0 - BETA_ONE) * clipped
    variance_new = BETA_TWO * variance + (1.0 - BETA_TWO) * clipped * clipped
    step_size = STEP_SCALE * width_all ** (-0.5)
    updated = (master_weight - step_size * moment_new / (jnp.sqrt(variance_new) + 1e-08)).astype(
        jnp.bfloat16
    )
    updated = updated.reshape(slab_rows, slab_heads * head_size)
    home = jnp.stack([to_column(updated, 0), to_column(updated, 1)])
    home = jnp.stack([home, swap(home, "core")])
    first = onward(home)
    first, gathered = lax.optimization_barrier((first, gathered))

    square = squares(8, gathered)
    other_square = swap(square, "xh")
    gain = lax.dynamic_index_in_dim(norm_gain.reshape(8, 2, width_part), xh, 1, False).reshape(-1, 1)
    place = (((((steps >> 1) & 1) ^ core) * 2 + ((steps >> 2) ^ xl)) * 2 + (steps & 1)).astype(jnp.int32)
    normed = normalise(float(width_all), 8, place, square, other_square, gain, gathered)

    second = onward(first)
    third = onward(second)
    early = swap(jnp.stack([first, second]), "core")
    last = onward(third[0])
    last, normed = lax.optimization_barrier((last, normed))
    late = swap(jnp.concatenate([third, last[None]]), "core")

    up = 1 - 2 * core
    source = (y - up * jnp.where(steps < 5, steps, 4 - steps)) & 7
    native = ((source >> 1) & 1) == xh
    origin = jnp.where(native, source, (source + 2 * (source & 1) - 1) & 7)
    slab = jnp.where(native, xh, 1 - xh)
    place = jnp.stack([(origin >> 2) * 2 + (origin & 1), slab ^ xh, slab]).astype(jnp.int32)
    weight = assemble(place, home, first, second, third, last, early, late)

    tables = rope_tables(seq_rows, head_size)
    gain_row = lax.dynamic_slice_in_dim(key_gain, z, 1, 0)
    query_cols = (slab_heads - 1) * head_size
    part = seq_rows // 2

    def product(rows, weight):
        return lax.dot_general(rows, weight, (((0,), (0,)), ((), ())), preferred_element_type=jnp.float32)

    result = ()
    for start in range(0, seq_rows, part):
        partial = product(normed[:, start : start + part], weight)
        got = swap(partial[:, query_cols:].astype(jnp.bfloat16), "xh")
        result = attend(prompt_len, partial, got, query_gain, gain_row, tables, tuple(result))
    return result[0]


def solution(mesh):
    fine = Mesh(mesh.devices.reshape(SIZES), AXES)
    rows, cols = ("xl", "core", "y"), ("z", "xh")
    slab = P(rows, cols, None, None)
    in_specs = (P(rows, cols), P(), slab, slab, slab, slab, P(cols, None), P(), P(rows))
    return jax.shard_map(
        shards, mesh=fine, in_specs=in_specs, out_specs=P(rows, cols), check_vma=False
    )
```

```python
import functools

import jax
import jax.numpy as jnp
import numpy as np
from jax import lax
from jax.experimental import pallas as pl
from jax.experimental.pallas import tpu as pltpu
from jax.sharding import Mesh, PartitionSpec as P

STEP_SCALE = 0.5
BETA_ONE = 0.9
BETA_TWO = 0.95
ROPE_BASE = 500000.0
AXES = ("xl", "core", "y", "z", "xh")
SIZES = (2, 2, 8, 8, 2)


def rope_tables(length, head_size):
    exponent = np.arange(head_size // 2, dtype=np.float32) * np.float32(2.0) / head_size
    inverse = np.power(np.float64(ROPE_BASE), -exponent.astype(np.float64)).astype(np.float32)
    angles = np.arange(length, dtype=np.float32)[:, None] * inverse[None, :]
    cosine = np.cos(angles.astype(np.float64)).astype(np.float32)
    sine = np.sin(angles.astype(np.float64)).astype(np.float32)
    return np.concatenate([cosine, cosine], axis=1), np.concatenate([-sine, sine], axis=1)


def rms_rotated(inputs, gain, cosine, sine):
    scale = lax.rsqrt(jnp.mean(inputs * inputs, axis=-1, keepdims=True) + 1e-06)
    scaled = inputs * scale * gain
    return scaled * cosine + pltpu.roll(scaled, scaled.shape[-1] // 2, 1) * sine


VMEM = pl.BlockSpec(memory_space=pltpu.VMEM)
SMEM = pl.BlockSpec(memory_space=pltpu.SMEM)


def local_call(kernel, name, out_shape, in_specs, out_specs):
    params = pltpu.CompilerParams(vmem_limit_bytes=8 << 20)
    return pl.pallas_call(
        kernel, out_shape=out_shape, in_specs=in_specs, out_specs=out_specs, compiler_params=params, name=name
    )


def assemble_kernel(place_ref, home_ref, *refs):
    *step_refs, last_ref, early_ref, late_ref, own_ref, sent_ref = refs
    _, _, rows, cols = home_ref.shape
    head = own_ref.shape[1] // 4
    wide = cols - head

    def put(step, lane, block_ref, *index):
        row = pl.multiple_of(place_ref[0, step] * rows, 32)
        pair_col = pl.multiple_of(wide + place_ref[2, step] * head, 128)
        spans = [pl.ds((lane * 2 + near) * 4 * rows + row, rows) for near in range(2)]

        def put_queries(out_ref):
            for near, span in enumerate(spans):
                out_ref[span, :wide] = block_ref[*index, near, :, :wide]

        pl.when(place_ref[1, step] == 0)(lambda: put_queries(own_ref))
        pl.when(place_ref[1, step] == 1)(lambda: put_queries(sent_ref))
        for near, span in enumerate(spans):
            pair = block_ref[*index, near, :, wide:]
            own_ref[span, pl.ds(pair_col, head)] = pair
            sent_ref[span, pl.ds(pair_col, head)] = pair

    for lane in range(2):
        put(0, lane, home_ref, lane)
        for step in range(3):
            put(1 + step, lane, step_refs[step], lane)
        for step in range(2):
            put(5 + step, 1 - lane, early_ref, step, lane)
        put(7, 1 - lane, late_ref, lane)
    put(4, 0, last_ref)
    put(4, 1, late_ref, 2)


def assemble(place, home, *rest):
    _, _, rows, cols = home.shape
    shape = [jax.ShapeDtypeStruct((16 * rows, 4 * cols // 3), home.dtype)] * 2
    call = local_call(assemble_kernel, "assemble", shape, [SMEM] + [VMEM] * (1 + len(rest)), [VMEM] * 2)
    return call(place, home, *rest)


def squares_kernel(parts, features_ref, out_ref):
    rows = features_ref.shape[0] // parts
    total = None
    for step in range(parts):
        wide = features_ref[step * rows : (step + 1) * rows, :].astype(jnp.float32)
        square = jnp.sum(wide * wide, axis=0, keepdims=True)
        total = square if total is None else total + square
    out_ref[...] = total


def squares(parts, features):
    shape = jax.ShapeDtypeStruct((1, features.shape[1]), jnp.float32)
    return local_call(functools.partial(squares_kernel, parts), "squares", shape, [VMEM], VMEM)(features)


def normalise_kernel(width_all, parts, place_ref, square_ref, other_ref, gain_ref, features_ref, out_ref):
    rows = features_ref.shape[0] // parts
    scale = lax.rsqrt((square_ref[...] + other_ref[...]) / width_all + 1e-06)
    for step in range(parts):
        span = slice(step * rows, (step + 1) * rows)
        row = pl.multiple_of(place_ref[step] * rows, 64)
        scaled = features_ref[span, :].astype(jnp.float32) * scale * gain_ref[span, :]
        out_ref[pl.ds(row, rows), :] = scaled.astype(out_ref.dtype)


def normalise(width_all, parts, place, square, other, gain, features):
    shape = jax.ShapeDtypeStruct(features.shape, jnp.bfloat16)
    kernel = functools.partial(normalise_kernel, width_all, parts)
    call = local_call(kernel, "normalise", shape, [SMEM] + [VMEM] * 4, VMEM)
    return call(place, square, other, gain, features)


def attend_kernel(tile, first, limit_ref, own_ref, got_ref, query_gain_ref, key_gain_ref, cos_ref, sin_ref, *refs):
    before, out_ref, keys_ref, values_ref = refs[:-3], *refs[-3:]
    heads, head = query_gain_ref.shape
    wide = heads * head
    limit = limit_ref[0]
    rows = own_ref.shape[0]
    if before:
        out_ref[:first, :] = before[0][...]
        keys_ref[:first, :] = before[1][...]
        values_ref[:first, :] = before[2][...]

    def summed(start, size, col):
        got = got_ref[start : start + size, col : col + head].astype(jnp.float32)
        return own_ref[start : start + size, col : col + head] + got

    cosine, sine = cos_ref[first : first + rows, :], sin_ref[first : first + rows, :]
    keys = rms_rotated(summed(0, rows, wide), key_gain_ref[...], cosine, sine)
    keys_ref[first:, :] = keys.astype(jnp.bfloat16)
    values_ref[first:, :] = summed(0, rows, wide + head).astype(jnp.bfloat16)
    for start in range(0, rows, tile):
        seen = first + start + tile
        row = first + start + lax.broadcasted_iota(jnp.int32, (tile, seen), 0)
        col = lax.broadcasted_iota(jnp.int32, (tile, seen), 1)
        allowed = (col <= row) & (col < limit)
        cosine, sine = cos_ref[first + start : seen, :], sin_ref[first + start : seen, :]
        for j in range(heads):
            projected = summed(start, tile, j * head)
            query = rms_rotated(projected, query_gain_ref[j : j + 1, :], cosine, sine)
            query = (query * head**-0.5).astype(jnp.bfloat16)
            scores = lax.dot_general(
                query, keys_ref[:seen, :], (((1,), (1,)), ((), ())), preferred_element_type=jnp.float32
            )
            scores = jnp.where(allowed, scores, -1e30)
            weights = jnp.exp(scores - jnp.max(scores, axis=-1, keepdims=True))
            weights = weights / jnp.sum(weights, axis=-1, keepdims=True)
            output = jnp.dot(weights.astype(jnp.bfloat16), values_ref[:seen, :], preferred_element_type=jnp.float32)
            out_ref[first + start : seen, j * head : (j + 1) * head] = output.astype(out_ref.dtype)


def attend(limit, own, got, query_gain, key_gain, tables, before):
    rows = own.shape[0]
    heads, head = query_gain.shape
    first = before[0].shape[0] if before else 0
    shape = [jax.ShapeDtypeStruct((first + rows, n), jnp.bfloat16) for n in (heads * head, head, head)]
    kernel = functools.partial(attend_kernel, rows // 2, first)
    call = local_call(kernel, "attend", shape, [SMEM] + [VMEM] * (6 + len(before)), [VMEM] * 3)
    return call(limit, own, got, query_gain, key_gain, *tables, *before)


def swap(array, axis):
    return lax.ppermute(array, axis, [(0, 1), (1, 0)])


def global_sum(value):
    count = 1
    for size in SIZES:
        count *= size
    spread = jnp.broadcast_to(value, (count, 128))
    return jnp.sum(lax.all_to_all(spread, AXES, 0, 0, tiled=True)[:, 0])


def to_column(block, other):
    pairs = []
    for xl in range(2):
        for y in range(8):
            for slab in range(2):
                column = (y >> 1) % 2
                target = y if slab == column else (y + (1 if y % 2 else -1)) % 8
                pairs.append(((xl * 8 + y) * 2 + slab, ((xl ^ other) * 8 + target) * 2 + column))
    return lax.ppermute(block, ("xl", "y", "xh"), pairs)


def onward(block):
    pairs = [(y, (y + 1) % 8) for y in range(8)] + [(8 + y, 8 + (y - 1) % 8) for y in range(8)]
    return lax.ppermute(block, ("core", "y"), pairs)


def shards(
    activations, norm_gain, master_weight, grad, moment, variance, query_gain, key_gain, prompt_len
):
    xl, core, y, z, xh = (lax.axis_index(a) for a in AXES)
    width_all = norm_gain.shape[0]
    seq_rows, width_part = activations.shape
    slab_rows, _, slab_heads, head_size = grad.shape
    steps = jnp.arange(8)

    gathered = lax.all_gather(activations.T, "z", axis=0, tiled=True)

    grad_local = grad.astype(jnp.float32)
    sumsq = global_sum(jnp.sum(grad_local * grad_local))
    clip_factor = 1.0 / jnp.sqrt(sumsq + 1e-12)
    clipped = grad_local * clip_factor
    moment_new = BETA_ONE * moment + (1.0 - BETA_ONE) * clipped
    variance_new = BETA_TWO * variance + (1.0 - BETA_TWO) * clipped * clipped
    step_size = STEP_SCALE * width_all ** (-0.5)
    updated = (master_weight - step_size * moment_new / (jnp.sqrt(variance_new) + 1e-08)).astype(
        jnp.bfloat16
    )
    updated = updated.reshape(slab_rows, slab_heads * head_size)
    home = jnp.stack([to_column(updated, 0), to_column(updated, 1)])
    home = jnp.stack([home, swap(home, "core")])
    first = onward(home)
    first, gathered = lax.optimization_barrier((first, gathered))

    square = squares(8, gathered)
    second = onward(first)
    second, square = lax.optimization_barrier((second, square))
    other_square = swap(square, "xh")
    gain = lax.dynamic_index_in_dim(norm_gain.reshape(8, 2, width_part), xh, 1, False).reshape(-1, 1)
    place = (((((steps >> 1) & 1) ^ core) * 2 + ((steps >> 2) ^ xl)) * 2 + (steps & 1)).astype(jnp.int32)
    normed = normalise(float(width_all), 8, place, square, other_square, gain, gathered)

    third = onward(second)
    third, normed = lax.optimization_barrier((third, normed))
    early = swap(jnp.stack([first, second]), "core")
    last = onward(third[0])
    late = swap(jnp.concatenate([third, last[None]]), "core")

    up = 1 - 2 * core
    source = (y - up * jnp.where(steps < 5, steps, 4 - steps)) & 7
    native = ((source >> 1) & 1) == xh
    origin = jnp.where(native, source, (source + 2 * (source & 1) - 1) & 7)
    slab = jnp.where(native, xh, 1 - xh)
    place = jnp.stack([(origin >> 2) * 2 + (origin & 1), slab ^ xh, slab]).astype(jnp.int32)
    own_weight, sent_weight = assemble(place, home, first, second, third, last, early, late)

    tables = rope_tables(seq_rows, head_size)
    gain_row = lax.dynamic_slice_in_dim(key_gain, z, 1, 0)
    part = seq_rows // 2

    def product(start, weight):
        rows = normed[:, start : start + part]
        return lax.dot_general(rows, weight, (((0,), (0,)), ((), ())), preferred_element_type=jnp.float32)

    starts = range(0, seq_rows, part)
    got = [swap(product(start, sent_weight).astype(jnp.bfloat16), "xh") for start in starts]
    result = ()
    for start, other in zip(starts, got):
        own = product(start, own_weight)
        result = attend(prompt_len, own, other, query_gain, gain_row, tables, tuple(result))
    return result[0]


def solution(mesh):
    fine = Mesh(mesh.devices.reshape(SIZES), AXES)
    rows, cols = ("xl", "core", "y"), ("z", "xh")
    slab = P(rows, cols, None, None)
    in_specs = (P(rows, cols), P(), slab, slab, slab, slab, P(cols, None), P(), P(rows))
    return jax.shard_map(
        shards, mesh=fine, in_specs=in_specs, out_specs=P(rows, cols), check_vma=False
    )
```

```python
import functools

import jax
import jax.numpy as jnp
import numpy as np
from jax import lax
from jax.experimental import pallas as pl
from jax.experimental.pallas import tpu as pltpu
from jax.sharding import Mesh, PartitionSpec as P

STEP_SCALE = 0.5
BETA_ONE = 0.9
BETA_TWO = 0.95
ROPE_BASE = 500000.0
AXES = ("xl", "core", "y", "z", "xh")
SIZES = (2, 2, 8, 8, 2)


def rope_tables(length, head_size):
    exponent = np.arange(head_size // 2, dtype=np.float32) * np.float32(2.0) / head_size
    inverse = np.power(np.float64(ROPE_BASE), -exponent.astype(np.float64)).astype(np.float32)
    angles = np.arange(length, dtype=np.float32)[:, None] * inverse[None, :]
    cosine = np.cos(angles.astype(np.float64)).astype(np.float32)
    sine = np.sin(angles.astype(np.float64)).astype(np.float32)
    return np.concatenate([cosine, cosine], axis=1), np.concatenate([-sine, sine], axis=1)


def rms_rotated(inputs, gain, cosine, sine):
    scale = lax.rsqrt(jnp.mean(inputs * inputs, axis=-1, keepdims=True) + 1e-06)
    scaled = inputs * scale * gain
    return scaled * cosine + pltpu.roll(scaled, scaled.shape[-1] // 2, 1) * sine


VMEM = pl.BlockSpec(memory_space=pltpu.VMEM)
SMEM = pl.BlockSpec(memory_space=pltpu.SMEM)


def local_call(kernel, name, out_shape, in_specs, out_specs):
    params = pltpu.CompilerParams(vmem_limit_bytes=8 << 20)
    return pl.pallas_call(
        kernel, out_shape=out_shape, in_specs=in_specs, out_specs=out_specs, compiler_params=params, name=name
    )


def assemble_kernel(place_ref, ring_place_ref, gathered_ref, swapped_ref, home_ref, *refs):
    *step_refs, last_ref, early_ref, late_ref, own_ref, sent_ref = refs
    parts, rows, cols = gathered_ref.shape
    head = own_ref.shape[1] // 4
    wide = cols - head

    def put(table_ref, step, lane, near, block_ref, *index):
        row = pl.multiple_of(table_ref[0, step] * rows, 32)
        pair_col = pl.multiple_of(wide + table_ref[2, step] * head, 128)
        span = pl.ds((lane * 2 + near) * 4 * rows + row, rows)

        def put_queries(out_ref):
            out_ref[span, :wide] = block_ref[*index, :, :wide]

        pl.when(table_ref[1, step] == 0)(lambda: put_queries(own_ref))
        pl.when(table_ref[1, step] == 1)(lambda: put_queries(sent_ref))
        pair = block_ref[*index, :, wide:]
        own_ref[span, pl.ds(pair_col, head)] = pair
        sent_ref[span, pl.ds(pair_col, head)] = pair

    for step in range(parts):
        put(place_ref, step, 0, 0, gathered_ref, step)
        put(place_ref, step, 1, 0, swapped_ref, step)
    for lane in range(2):
        put(ring_place_ref, 0, lane, 1, home_ref, lane)
        for step in range(3):
            put(ring_place_ref, 1 + step, lane, 1, step_refs[step], lane)
        for step in range(2):
            put(ring_place_ref, 5 + step, 1 - lane, 1, early_ref, step, lane)
        put(ring_place_ref, 7, 1 - lane, 1, late_ref, lane)
    put(ring_place_ref, 4, 0, 1, last_ref)
    put(ring_place_ref, 4, 1, 1, late_ref, 2)


def assemble(place, ring_place, gathered, *rest):
    parts, rows, cols = gathered.shape
    shape = [jax.ShapeDtypeStruct((4 * parts // 2 * rows, 4 * cols // 3), gathered.dtype)] * 2
    call = local_call(assemble_kernel, "assemble", shape, [SMEM] * 2 + [VMEM] * (1 + len(rest)), [VMEM] * 2)
    return call(place, ring_place, gathered, *rest)


def squares_kernel(parts, features_ref, out_ref):
    rows = features_ref.shape[0] // parts
    total = None
    for step in range(parts):
        wide = features_ref[step * rows : (step + 1) * rows, :].astype(jnp.float32)
        square = jnp.sum(wide * wide, axis=0, keepdims=True)
        total = square if total is None else total + square
    out_ref[...] = total


def squares(parts, features):
    shape = jax.ShapeDtypeStruct((1, features.shape[1]), jnp.float32)
    return local_call(functools.partial(squares_kernel, parts), "squares", shape, [VMEM], VMEM)(features)


def normalise_kernel(width_all, parts, place_ref, square_ref, other_ref, gain_ref, features_ref, out_ref):
    rows = features_ref.shape[0] // parts
    scale = lax.rsqrt((square_ref[...] + other_ref[...]) / width_all + 1e-06)
    for step in range(parts):
        span = slice(step * rows, (step + 1) * rows)
        row = pl.multiple_of(place_ref[step] * rows, 64)
        scaled = features_ref[span, :].astype(jnp.float32) * scale * gain_ref[span, :]
        out_ref[pl.ds(row, rows), :] = scaled.astype(out_ref.dtype)


def normalise(width_all, parts, place, square, other, gain, features):
    shape = jax.ShapeDtypeStruct(features.shape, jnp.bfloat16)
    kernel = functools.partial(normalise_kernel, width_all, parts)
    call = local_call(kernel, "normalise", shape, [SMEM] + [VMEM] * 4, VMEM)
    return call(place, square, other, gain, features)


def attend_kernel(tile, first, limit_ref, own_ref, got_ref, query_gain_ref, key_gain_ref, cos_ref, sin_ref, *refs):
    before, out_ref, keys_ref, values_ref = refs[:-3], *refs[-3:]
    heads, head = query_gain_ref.shape
    wide = heads * head
    limit = limit_ref[0]
    rows = own_ref.shape[0]
    if before:
        out_ref[:first, :] = before[0][...]
        keys_ref[:first, :] = before[1][...]
        values_ref[:first, :] = before[2][...]

    def summed(start, size, col):
        got = got_ref[start : start + size, col : col + head].astype(jnp.float32)
        return own_ref[start : start + size, col : col + head] + got

    cosine, sine = cos_ref[first : first + rows, :], sin_ref[first : first + rows, :]
    keys = rms_rotated(summed(0, rows, wide), key_gain_ref[...], cosine, sine)
    keys_ref[first:, :] = keys.astype(jnp.bfloat16)
    values_ref[first:, :] = summed(0, rows, wide + head).astype(jnp.bfloat16)
    for start in range(0, rows, tile):
        seen = first + start + tile
        row = first + start + lax.broadcasted_iota(jnp.int32, (tile, seen), 0)
        col = lax.broadcasted_iota(jnp.int32, (tile, seen), 1)
        allowed = (col <= row) & (col < limit)
        cosine, sine = cos_ref[first + start : seen, :], sin_ref[first + start : seen, :]
        for j in range(heads):
            projected = summed(start, tile, j * head)
            query = rms_rotated(projected, query_gain_ref[j : j + 1, :], cosine, sine)
            query = (query * head**-0.5).astype(jnp.bfloat16)
            scores = lax.dot_general(
                query, keys_ref[:seen, :], (((1,), (1,)), ((), ())), preferred_element_type=jnp.float32
            )
            scores = jnp.where(allowed, scores, -1e30)
            weights = jnp.exp(scores - jnp.max(scores, axis=-1, keepdims=True))
            weights = weights / jnp.sum(weights, axis=-1, keepdims=True)
            output = jnp.dot(weights.astype(jnp.bfloat16), values_ref[:seen, :], preferred_element_type=jnp.float32)
            out_ref[first + start : seen, j * head : (j + 1) * head] = output.astype(out_ref.dtype)


def attend(limit, own, got, query_gain, key_gain, tables, before):
    rows = own.shape[0]
    heads, head = query_gain.shape
    first = before[0].shape[0] if before else 0
    shape = [jax.ShapeDtypeStruct((first + rows, n), jnp.bfloat16) for n in (heads * head, head, head)]
    kernel = functools.partial(attend_kernel, rows // 2, first)
    call = local_call(kernel, "attend", shape, [SMEM] + [VMEM] * (6 + len(before)), [VMEM] * 3)
    return call(limit, own, got, query_gain, key_gain, *tables, *before)


def swap(array, axis):
    return lax.ppermute(array, axis, [(0, 1), (1, 0)])


def global_sum(value):
    count = 1
    for size in SIZES:
        count *= size
    spread = jnp.broadcast_to(value, (count, 128))
    return jnp.sum(lax.all_to_all(spread, AXES, 0, 0, tiled=True)[:, 0])


def to_column(block, other):
    pairs = []
    for xl in range(2):
        for y in range(8):
            for slab in range(2):
                column = (y >> 1) % 2
                target = y if slab == column else (y + (1 if y % 2 else -1)) % 8
                pairs.append(((xl * 8 + y) * 2 + slab, ((xl ^ other) * 8 + target) * 2 + column))
    return lax.ppermute(block, ("xl", "y", "xh"), pairs)


def onward(block):
    pairs = [(y, (y + 1) % 8) for y in range(8)] + [(8 + y, 8 + (y - 1) % 8) for y in range(8)]
    return lax.ppermute(block, ("core", "y"), pairs)


def shards(
    activations, norm_gain, master_weight, grad, moment, variance, query_gain, key_gain, prompt_len
):
    xl, core, y, z, xh = (lax.axis_index(a) for a in AXES)
    width_all = norm_gain.shape[0]
    seq_rows, width_part = activations.shape
    slab_rows, _, slab_heads, head_size = grad.shape
    steps = jnp.arange(8)

    gathered = lax.all_gather(activations.T, "z", axis=0, tiled=True)

    grad_local = grad.astype(jnp.float32)
    sumsq = global_sum(jnp.sum(grad_local * grad_local))
    clip_factor = 1.0 / jnp.sqrt(sumsq + 1e-12)
    clipped = grad_local * clip_factor
    moment_new = BETA_ONE * moment + (1.0 - BETA_ONE) * clipped
    variance_new = BETA_TWO * variance + (1.0 - BETA_TWO) * clipped * clipped
    step_size = STEP_SCALE * width_all ** (-0.5)
    updated = (master_weight - step_size * moment_new / (jnp.sqrt(variance_new) + 1e-08)).astype(
        jnp.bfloat16
    )
    updated = updated.reshape(slab_rows, slab_heads * head_size)
    arrived = lax.all_gather(to_column(updated, 0), "y", axis=0)
    home = to_column(updated, 1)
    home = jnp.stack([home, swap(home, "core")])
    first = onward(home)
    first, gathered = lax.optimization_barrier((first, gathered))

    square = squares(8, gathered)
    second = onward(first)
    second, square = lax.optimization_barrier((second, square))
    other_square = swap(square, "xh")
    gain = lax.dynamic_index_in_dim(norm_gain.reshape(8, 2, width_part), xh, 1, False).reshape(-1, 1)
    place = (((((steps >> 1) & 1) ^ core) * 2 + ((steps >> 2) ^ xl)) * 2 + (steps & 1)).astype(jnp.int32)
    normed = normalise(float(width_all), 8, place, square, other_square, gain, gathered)

    third = onward(second)
    third, normed = lax.optimization_barrier((third, normed))
    early = swap(jnp.stack([first, second]), "core")
    last = onward(third[0])
    last, arrived = lax.optimization_barrier((last, arrived))
    late = swap(jnp.concatenate([third, last[None]]), "core")

    def place_of(source):
        native = ((source >> 1) & 1) == xh
        origin = jnp.where(native, source, (source + 2 * (source & 1) - 1) & 7)
        slab = jnp.where(native, xh, 1 - xh)
        return jnp.stack([(origin >> 2) * 2 + (origin & 1), slab ^ xh, slab]).astype(jnp.int32)

    ring_source = (y - (1 - 2 * core) * jnp.where(steps < 5, steps, 4 - steps)) & 7
    own_weight, sent_weight = assemble(
        place_of(steps), place_of(ring_source), arrived, swap(arrived, "core"), home, first, second, third, last, early, late
    )

    tables = rope_tables(seq_rows, head_size)
    gain_row = lax.dynamic_slice_in_dim(key_gain, z, 1, 0)
    part = seq_rows // 2

    def product(start, weight):
        rows = normed[:, start : start + part]
        return lax.dot_general(rows, weight, (((0,), (0,)), ((), ())), preferred_element_type=jnp.float32)

    starts = range(0, seq_rows, part)
    got = [swap(product(start, sent_weight).astype(jnp.bfloat16), "xh") for start in starts]
    result = ()
    for start, other in zip(starts, got):
        own = product(start, own_weight)
        result = attend(prompt_len, own, other, query_gain, gain_row, tables, tuple(result))
    return result[0]


def solution(mesh):
    fine = Mesh(mesh.devices.reshape(SIZES), AXES)
    rows, cols = ("xl", "core", "y"), ("z", "xh")
    slab = P(rows, cols, None, None)
    in_specs = (P(rows, cols), P(), slab, slab, slab, slab, P(cols, None), P(), P(rows))
    return jax.shard_map(
        shards, mesh=fine, in_specs=in_specs, out_specs=P(rows, cols), check_vma=False
    )
```

```python
import functools

import jax
import jax.numpy as jnp
import numpy as np
from jax import lax
from jax.experimental import pallas as pl
from jax.experimental.pallas import tpu as pltpu
from jax.sharding import Mesh, PartitionSpec as P

STEP_SCALE = 0.5
BETA_ONE = 0.9
BETA_TWO = 0.95
ROPE_BASE = 500000.0
AXES = ("xl", "core", "y", "z", "xh")
SIZES = (2, 2, 8, 8, 2)


def rope_tables(length, head_size):
    exponent = np.arange(head_size // 2, dtype=np.float32) * np.float32(2.0) / head_size
    inverse = np.power(np.float64(ROPE_BASE), -exponent.astype(np.float64)).astype(np.float32)
    angles = np.arange(length, dtype=np.float32)[:, None] * inverse[None, :]
    cosine = np.cos(angles.astype(np.float64)).astype(np.float32)
    sine = np.sin(angles.astype(np.float64)).astype(np.float32)
    return np.concatenate([cosine, cosine], axis=1), np.concatenate([-sine, sine], axis=1)


def rms_rotated(inputs, gain, cosine, sine):
    scale = lax.rsqrt(jnp.mean(inputs * inputs, axis=-1, keepdims=True) + 1e-06)
    scaled = inputs * scale * gain
    return scaled * cosine + pltpu.roll(scaled, scaled.shape[-1] // 2, 1) * sine


VMEM = pl.BlockSpec(memory_space=pltpu.VMEM)
SMEM = pl.BlockSpec(memory_space=pltpu.SMEM)


def local_call(kernel, name, out_shape, in_specs, out_specs):
    return pl.pallas_call(
        kernel,
        out_shape=out_shape,
        in_specs=in_specs,
        out_specs=out_specs,
        compiler_params=pltpu.CompilerParams(vmem_limit_bytes=8 << 20),
        name=name,
    )


def put_block(place_ref, step, lane, block_ref, index, own_ref, sent_ref):
    rows, cols = block_ref.shape[-2:]
    head = own_ref.shape[1] // 4
    wide = cols - head
    row = pl.multiple_of(place_ref[0, step] * rows, 32)
    pair_col = pl.multiple_of(wide + place_ref[2, step] * head, 128)
    spans = [pl.ds((lane * 2 + near) * 4 * rows + row, rows) for near in range(2)]

    def put_queries(out_ref):
        for near, span in enumerate(spans):
            out_ref[span, :wide] = block_ref[*index, near, :, :wide]

    pl.when(place_ref[1, step] == 0)(lambda: put_queries(own_ref))
    pl.when(place_ref[1, step] == 1)(lambda: put_queries(sent_ref))
    for near, span in enumerate(spans):
        pair = block_ref[*index, near, :, wide:]
        own_ref[span, pl.ds(pair_col, head)] = pair
        sent_ref[span, pl.ds(pair_col, head)] = pair


def assemble_kernel(place_ref, home_ref, first_ref, second_ref, third_ref, early_ref, last_ref, final_ref, *outs):
    for lane in range(2):
        for step, block_ref in enumerate((home_ref, first_ref, second_ref, third_ref)):
            put_block(place_ref, step, lane, block_ref, (lane,), *outs)
        for step in range(3):
            put_block(place_ref, 5 + step, 1 - lane, early_ref, (step, lane), *outs)
    put_block(place_ref, 4, 0, last_ref, (), *outs)
    put_block(place_ref, 4, 1, final_ref, (), *outs)


def assemble(place, home, *rest):
    _, _, rows, cols = home.shape
    shape = [jax.ShapeDtypeStruct((16 * rows, 4 * cols // 3), home.dtype)] * 2
    call = local_call(assemble_kernel, "assemble", shape, [SMEM] + [VMEM] * (1 + len(rest)), [VMEM] * 2)
    return call(place, home, *rest)


def squares_kernel(parts, features_ref, out_ref):
    rows = features_ref.shape[0] // parts
    total = None
    for step in range(parts):
        wide = features_ref[step * rows : (step + 1) * rows, :].astype(jnp.float32)
        square = jnp.sum(wide * wide, axis=0, keepdims=True)
        total = square if total is None else total + square
    out_ref[...] = total


def squares(parts, features):
    shape = jax.ShapeDtypeStruct((1, features.shape[1]), jnp.float32)
    return local_call(functools.partial(squares_kernel, parts), "squares", shape, [VMEM], VMEM)(features)


def normalise_kernel(width_all, parts, place_ref, square_ref, other_ref, gain_ref, features_ref, out_ref):
    rows = features_ref.shape[0] // parts
    scale = lax.rsqrt((square_ref[...] + other_ref[...]) / width_all + 1e-06)
    for step in range(parts):
        span = slice(step * rows, (step + 1) * rows)
        row = pl.multiple_of(place_ref[step] * rows, 64)
        scaled = features_ref[span, :].astype(jnp.float32) * scale * gain_ref[span, :]
        out_ref[pl.ds(row, rows), :] = scaled.astype(out_ref.dtype)


def normalise(width_all, parts, place, square, other, gain, features):
    shape = jax.ShapeDtypeStruct(features.shape, jnp.bfloat16)
    kernel = functools.partial(normalise_kernel, width_all, parts)
    call = local_call(kernel, "normalise", shape, [SMEM] + [VMEM] * 4, VMEM)
    return call(place, square, other, gain, features)


def attend_kernel(tile, first, limit_ref, own_ref, got_ref, query_gain_ref, key_gain_ref, cos_ref, sin_ref, *refs):
    before, out_ref, keys_ref, values_ref = refs[:-3], *refs[-3:]
    heads, head = query_gain_ref.shape
    wide = heads * head
    limit = limit_ref[0]
    rows = own_ref.shape[0]
    if before:
        out_ref[:first, :] = before[0][...]
        keys_ref[:first, :] = before[1][...]
        values_ref[:first, :] = before[2][...]

    def summed(start, size, col):
        got = got_ref[start : start + size, col : col + head].astype(jnp.float32)
        return own_ref[start : start + size, col : col + head] + got

    cosine, sine = cos_ref[first : first + rows, :], sin_ref[first : first + rows, :]
    keys = rms_rotated(summed(0, rows, wide), key_gain_ref[...], cosine, sine)
    keys_ref[first:, :] = keys.astype(jnp.bfloat16)
    values_ref[first:, :] = summed(0, rows, wide + head).astype(jnp.bfloat16)
    for start in range(0, rows, tile):
        seen = first + start + tile
        row = first + start + lax.broadcasted_iota(jnp.int32, (tile, seen), 0)
        col = lax.broadcasted_iota(jnp.int32, (tile, seen), 1)
        allowed = (col <= row) & (col < limit)
        cosine, sine = cos_ref[first + start : seen, :], sin_ref[first + start : seen, :]
        for j in range(heads):
            projected = summed(start, tile, j * head)
            query = rms_rotated(projected, query_gain_ref[j : j + 1, :], cosine, sine)
            query = (query * head**-0.5).astype(jnp.bfloat16)
            scores = lax.dot_general(
                query, keys_ref[:seen, :], (((1,), (1,)), ((), ())), preferred_element_type=jnp.float32
            )
            scores = jnp.where(allowed, scores, -1e30)
            weights = jnp.exp(scores - jnp.max(scores, axis=-1, keepdims=True))
            weights = weights * (1.0 / jnp.sum(weights, axis=-1, keepdims=True))
            output = jnp.dot(weights.astype(jnp.bfloat16), values_ref[:seen, :], preferred_element_type=jnp.float32)
            out_ref[first + start : seen, j * head : (j + 1) * head] = output.astype(out_ref.dtype)


def attend(limit, own, got, query_gain, key_gain, tables, before):
    rows = own.shape[0]
    heads, head = query_gain.shape
    first = before[0].shape[0] if before else 0
    shape = [jax.ShapeDtypeStruct((first + rows, n), jnp.bfloat16) for n in (heads * head, head, head)]
    kernel = functools.partial(attend_kernel, min(rows, 256), first)
    call = local_call(kernel, "attend", shape, [SMEM] + [VMEM] * (6 + len(before)), [VMEM] * 3)
    return call(limit, own, got, query_gain, key_gain, *tables, *before)


def swap(array, axis):
    return lax.ppermute(array, axis, [(0, 1), (1, 0)])


def global_sum(value):
    count = 1
    for size in SIZES:
        count *= size
    spread = jnp.broadcast_to(value, (count, 128))
    return jnp.sum(lax.all_to_all(spread, AXES, 0, 0, tiled=True)[:, 0])


def to_column(block, other):
    pairs = []
    for xl in range(2):
        for y in range(8):
            for slab in range(2):
                column = (y >> 1) % 2
                target = y if slab == column else (y + (1 if y % 2 else -1)) % 8
                pairs.append(((xl * 8 + y) * 2 + slab, ((xl ^ other) * 8 + target) * 2 + column))
    return lax.ppermute(block, ("xl", "y", "xh"), pairs)


def onward(block):
    pairs = [(y, (y + 1) % 8) for y in range(8)] + [(8 + y, 8 + (y - 1) % 8) for y in range(8)]
    return lax.ppermute(block, ("core", "y"), pairs)


def shards(
    activations, norm_gain, master_weight, grad, moment, variance, query_gain, key_gain, prompt_len
):
    xl, core, y, z, xh = (lax.axis_index(a) for a in AXES)
    width_all = norm_gain.shape[0]
    seq_rows, width_part = activations.shape
    slab_rows, _, slab_heads, head_size = grad.shape
    steps = jnp.arange(8)

    gathered = lax.all_gather(activations.T, "z", axis=0, tiled=True)

    grad_local = grad.astype(jnp.float32)
    sumsq = global_sum(jnp.sum(grad_local * grad_local))
    flat = (slab_rows, slab_heads * head_size)
    flats = [array.reshape(flat) for array in (master_weight, moment, variance, grad)]
    gain = lax.dynamic_index_in_dim(norm_gain.reshape(8, 2, width_part), xh, 1, False).reshape(-1, 1)
    sumsq, gain, *flats = lax.optimization_barrier((sumsq, gain, *flats))
    master_flat, moment_flat, variance_flat, grad_flat = flats
    clip_factor = 1.0 / jnp.sqrt(sumsq + 1e-12)
    clipped = grad_flat.astype(jnp.float32) * clip_factor
    moment_new = BETA_ONE * moment_flat + (1.0 - BETA_ONE) * clipped
    variance_new = BETA_TWO * variance_flat + (1.0 - BETA_TWO) * clipped * clipped
    step_size = STEP_SCALE * width_all ** (-0.5)
    updated = (master_flat - step_size * moment_new / (jnp.sqrt(variance_new) + 1e-08)).astype(
        jnp.bfloat16
    )
    home = jnp.stack([to_column(updated, 0), to_column(updated, 1)])
    home = jnp.stack([home, swap(home, "core")])
    first = onward(home)
    first, gathered = lax.optimization_barrier((first, gathered))

    square = squares(8, gathered)
    other_square = swap(square, "xh")
    second = onward(first)
    second, other_square = lax.optimization_barrier((second, other_square))
    place = (((((steps >> 1) & 1) ^ core) * 2 + ((steps >> 2) ^ xl)) * 2 + (steps & 1)).astype(jnp.int32)
    normed = normalise(float(width_all), 8, place, square, other_square, gain, gathered)

    up = 1 - 2 * core
    source = (y - up * jnp.where(steps < 5, steps, 4 - steps)) & 7
    native = ((source >> 1) & 1) == xh
    origin = jnp.where(native, source, (source + 2 * (source & 1) - 1) & 7)
    slab = jnp.where(native, xh, 1 - xh)
    place = jnp.stack([(origin >> 2) * 2 + (origin & 1), slab ^ xh, slab]).astype(jnp.int32)

    third = onward(second)
    third, normed = lax.optimization_barrier((third, normed))
    last = onward(third[0])
    early = swap(jnp.stack([first, second, third]), "core")

    up = 1 - 2 * core
    source = (y - up * jnp.where(steps < 5, steps, 4 - steps)) & 7
    native = ((source >> 1) & 1) == xh
    origin = jnp.where(native, source, (source + 2 * (source & 1) - 1) & 7)
    slab = jnp.where(native, xh, 1 - xh)
    place = jnp.stack([(origin >> 2) * 2 + (origin & 1), slab ^ xh, slab]).astype(jnp.int32)
    own_weight, sent_weight = assemble(place, home, first, second, third, early, last, swap(last, "core"))

    tables = rope_tables(seq_rows, head_size)
    gain_row = lax.dynamic_slice_in_dim(key_gain, z, 1, 0)
    cut = seq_rows // 3 * 2

    def product(rows, weight):
        return lax.dot_general(rows, weight, (((0,), (0,)), ((), ())), preferred_element_type=jnp.float32)

    tokens = [normed[:, :cut], normed[:, cut:]]
    got = [swap(product(rows, sent_weight).astype(jnp.bfloat16), "xh") for rows in tokens]
    result = ()
    for rows, other in zip(tokens, got):
        own = product(rows, own_weight)
        result = attend(prompt_len, own, other, query_gain, gain_row, tables, tuple(result))
    return result[0]


def solution(mesh):
    fine = Mesh(mesh.devices.reshape(SIZES), AXES)
    rows, cols = ("xl", "core", "y"), ("z", "xh")
    slab = P(rows, cols, None, None)
    in_specs = (P(rows, cols), P(), slab, slab, slab, slab, P(cols, None), P(), P(rows))
    return jax.shard_map(
        shards, mesh=fine, in_specs=in_specs, out_specs=P(rows, cols), check_vma=False
    )
```

```python
import functools

import jax
import jax.numpy as jnp
import numpy as np
from jax import lax
from jax.experimental import pallas as pl
from jax.experimental.pallas import tpu as pltpu
from jax.sharding import Mesh, PartitionSpec as P

STEP_SCALE = 0.5
BETA_ONE = 0.9
BETA_TWO = 0.95
ROPE_BASE = 500000.0
AXES = ("xl", "core", "y", "z", "xh")
SIZES = (2, 2, 8, 8, 2)


def rope_tables(length, head_size):
    exponent = np.arange(head_size // 2, dtype=np.float32) * np.float32(2.0) / head_size
    inverse = np.power(np.float64(ROPE_BASE), -exponent.astype(np.float64)).astype(np.float32)
    angles = np.arange(length, dtype=np.float32)[:, None] * inverse[None, :]
    cosine = np.cos(angles.astype(np.float64)).astype(np.float32)
    sine = np.sin(angles.astype(np.float64)).astype(np.float32)
    return np.concatenate([cosine, cosine], axis=1), np.concatenate([-sine, sine], axis=1)


def rms_rotated(inputs, gain, cosine, sine):
    scale = lax.rsqrt(jnp.mean(inputs * inputs, axis=-1, keepdims=True) + 1e-06)
    scaled = inputs * scale * gain
    return scaled * cosine + pltpu.roll(scaled, scaled.shape[-1] // 2, 1) * sine


VMEM = pl.BlockSpec(memory_space=pltpu.VMEM)
SMEM = pl.BlockSpec(memory_space=pltpu.SMEM)


def local_call(kernel, name, out_shape, in_specs, out_specs):
    return pl.pallas_call(
        kernel,
        out_shape=out_shape,
        in_specs=in_specs,
        out_specs=out_specs,
        compiler_params=pltpu.CompilerParams(vmem_limit_bytes=8 << 20),
        name=name,
    )


def put_block(place_ref, step, lane, block_ref, index, own_ref, sent_ref):
    rows, cols = block_ref.shape[-2:]
    head = own_ref.shape[1] // 4
    wide = cols - head
    row = pl.multiple_of(place_ref[0, step] * rows, 32)
    pair_col = pl.multiple_of(wide + place_ref[2, step] * head, 128)
    spans = [pl.ds((lane * 2 + near) * 4 * rows + row, rows) for near in range(2)]

    def put_queries(out_ref):
        for near, span in enumerate(spans):
            out_ref[span, :wide] = block_ref[*index, near, :, :wide]

    pl.when(place_ref[1, step] == 0)(lambda: put_queries(own_ref))
    pl.when(place_ref[1, step] == 1)(lambda: put_queries(sent_ref))
    for near, span in enumerate(spans):
        pair = block_ref[*index, near, :, wide:]
        own_ref[span, pl.ds(pair_col, head)] = pair
        sent_ref[span, pl.ds(pair_col, head)] = pair


def assemble_kernel(place_ref, *refs):
    *block_refs, last_ref, final_ref, own_ref, sent_ref = refs
    outs = (own_ref, sent_ref)
    for lane in range(2):
        for step in range(4):
            put_block(place_ref, step, lane, block_refs[step], (lane,), *outs)
        for step in range(3):
            put_block(place_ref, 5 + step, 1 - lane, block_refs[4 + step], (lane,), *outs)
    put_block(place_ref, 4, 0, last_ref, (), *outs)
    put_block(place_ref, 4, 1, final_ref, (), *outs)


def assemble(place, home, *rest):
    _, _, rows, cols = home.shape
    shape = [jax.ShapeDtypeStruct((16 * rows, 4 * cols // 3), home.dtype)] * 2
    call = local_call(assemble_kernel, "assemble", shape, [SMEM] + [VMEM] * (1 + len(rest)), [VMEM] * 2)
    return call(place, home, *rest)


def squares_kernel(parts, features_ref, out_ref):
    rows = features_ref.shape[0] // parts
    total = None
    for step in range(parts):
        wide = features_ref[step * rows : (step + 1) * rows, :].astype(jnp.float32)
        square = jnp.sum(wide * wide, axis=0, keepdims=True)
        total = square if total is None else total + square
    out_ref[...] = total


def squares(parts, features):
    shape = jax.ShapeDtypeStruct((1, features.shape[1]), jnp.float32)
    return local_call(functools.partial(squares_kernel, parts), "squares", shape, [VMEM], VMEM)(features)


def normalise_kernel(width_all, parts, place_ref, square_ref, other_ref, gain_ref, features_ref, out_ref):
    rows = features_ref.shape[0] // parts
    scale = lax.rsqrt((square_ref[...] + other_ref[...]) / width_all + 1e-06)
    for step in range(parts):
        span = slice(step * rows, (step + 1) * rows)
        row = pl.multiple_of(place_ref[step] * rows, 64)
        scaled = features_ref[span, :].astype(jnp.float32) * scale * gain_ref[span, :]
        out_ref[pl.ds(row, rows), :] = scaled.astype(out_ref.dtype)


def normalise(width_all, parts, place, square, other, gain, features):
    shape = jax.ShapeDtypeStruct(features.shape, jnp.bfloat16)
    kernel = functools.partial(normalise_kernel, width_all, parts)
    call = local_call(kernel, "normalise", shape, [SMEM] + [VMEM] * 4, VMEM)
    return call(place, square, other, gain, features)


def attend_kernel(tile, first, limit_ref, own_ref, got_ref, query_gain_ref, key_gain_ref, cos_ref, sin_ref, *refs):
    before, out_ref, keys_ref, values_ref = refs[:-3], *refs[-3:]
    heads, head = query_gain_ref.shape
    wide = heads * head
    limit = limit_ref[0]
    rows = own_ref.shape[0]
    if before:
        out_ref[:first, :] = before[0][...]
        keys_ref[:first, :] = before[1][...]
        values_ref[:first, :] = before[2][...]

    def summed(start, size, col):
        got = got_ref[start : start + size, col : col + head].astype(jnp.float32)
        return own_ref[start : start + size, col : col + head] + got

    cosine, sine = cos_ref[first : first + rows, :], sin_ref[first : first + rows, :]
    keys = rms_rotated(summed(0, rows, wide), key_gain_ref[...], cosine, sine)
    keys_ref[first:, :] = keys.astype(jnp.bfloat16)
    values_ref[first:, :] = summed(0, rows, wide + head).astype(jnp.bfloat16)
    for start in range(0, rows, tile):
        seen = first + start + tile
        row = first + start + lax.broadcasted_iota(jnp.int32, (tile, seen), 0)
        col = lax.broadcasted_iota(jnp.int32, (tile, seen), 1)
        allowed = (col <= row) & (col < limit)
        cosine, sine = cos_ref[first + start : seen, :], sin_ref[first + start : seen, :]
        for j in range(heads):
            projected = summed(start, tile, j * head)
            query = rms_rotated(projected, query_gain_ref[j : j + 1, :], cosine, sine)
            query = (query * head**-0.5).astype(jnp.bfloat16)
            scores = lax.dot_general(
                query, keys_ref[:seen, :], (((1,), (1,)), ((), ())), preferred_element_type=jnp.float32
            )
            scores = jnp.where(allowed, scores, -1e30)
            weights = jnp.exp(scores - jnp.max(scores, axis=-1, keepdims=True))
            weights = weights * (1.0 / jnp.sum(weights, axis=-1, keepdims=True))
            output = jnp.dot(weights.astype(jnp.bfloat16), values_ref[:seen, :], preferred_element_type=jnp.float32)
            out_ref[first + start : seen, j * head : (j + 1) * head] = output.astype(out_ref.dtype)


def attend(limit, own, got, query_gain, key_gain, tables, before):
    rows = own.shape[0]
    heads, head = query_gain.shape
    first = before[0].shape[0] if before else 0
    shape = [jax.ShapeDtypeStruct((first + rows, n), jnp.bfloat16) for n in (heads * head, head, head)]
    kernel = functools.partial(attend_kernel, min(rows, 256), first)
    call = local_call(kernel, "attend", shape, [SMEM] + [VMEM] * (6 + len(before)), [VMEM] * 3)
    return call(limit, own, got, query_gain, key_gain, *tables, *before)


def swap(array, axis):
    return lax.ppermute(array, axis, [(0, 1), (1, 0)])


def global_sum(value):
    count = 1
    for size in SIZES:
        count *= size
    spread = jnp.broadcast_to(value, (count, 128))
    return jnp.sum(lax.all_to_all(spread, AXES, 0, 0, tiled=True)[:, 0])


def to_column(block, other):
    pairs = []
    for xl in range(2):
        for y in range(8):
            for slab in range(2):
                column = (y >> 1) % 2
                target = y if slab == column else (y + (1 if y % 2 else -1)) % 8
                pairs.append(((xl * 8 + y) * 2 + slab, ((xl ^ other) * 8 + target) * 2 + column))
    return lax.ppermute(block, ("xl", "y", "xh"), pairs)


def onward(block, steps):
    pairs = [(y, (y + steps) % 8) for y in range(8)] + [(8 + y, 8 + (y - steps) % 8) for y in range(8)]
    return lax.ppermute(block, ("core", "y"), pairs)


def shards(
    activations, norm_gain, master_weight, grad, moment, variance, query_gain, key_gain, prompt_len
):
    xl, core, y, z, xh = (lax.axis_index(a) for a in AXES)
    width_all = norm_gain.shape[0]
    seq_rows, width_part = activations.shape
    slab_rows, _, slab_heads, head_size = grad.shape
    steps = jnp.arange(8)

    gathered = lax.all_gather(activations.T, "z", axis=0, tiled=True)

    grad_local = grad.astype(jnp.float32)
    sumsq = global_sum(jnp.sum(grad_local * grad_local))
    flat = (slab_rows, slab_heads * head_size)
    flats = [array.reshape(flat) for array in (master_weight, moment, variance, grad)]
    gain = lax.dynamic_index_in_dim(norm_gain.reshape(8, 2, width_part), xh, 1, False).reshape(-1, 1)
    sumsq, gain, *flats = lax.optimization_barrier((sumsq, gain, *flats))
    master_flat, moment_flat, variance_flat, grad_flat = flats
    clip_factor = 1.0 / jnp.sqrt(sumsq + 1e-12)
    clipped = grad_flat.astype(jnp.float32) * clip_factor
    moment_new = BETA_ONE * moment_flat + (1.0 - BETA_ONE) * clipped
    variance_new = BETA_TWO * variance_flat + (1.0 - BETA_TWO) * clipped * clipped
    step_size = STEP_SCALE * width_all ** (-0.5)
    updated = (master_flat - step_size * moment_new / (jnp.sqrt(variance_new) + 1e-08)).astype(
        jnp.bfloat16
    )
    home = jnp.stack([to_column(updated, 0), to_column(updated, 1)])
    home = jnp.stack([home, swap(home, "core")])
    first, second = onward(home, 1), onward(home, 2)
    first, gathered = lax.optimization_barrier((first, gathered))
    exchanged = [swap(first, "core")]

    square = squares(8, gathered)
    second, square, exchanged[0] = lax.optimization_barrier((second, square, exchanged[0]))
    other_square = swap(square, "xh")
    place = (((((steps >> 1) & 1) ^ core) * 2 + ((steps >> 2) ^ xl)) * 2 + (steps & 1)).astype(jnp.int32)
    normed = normalise(float(width_all), 8, place, square, other_square, gain, gathered)

    third, last = onward(second, 1), onward(second[0], 2)
    third, normed = lax.optimization_barrier((third, normed))
    exchanged += [swap(second, "core"), swap(third, "core")]

    up = 1 - 2 * core
    source = (y - up * jnp.where(steps < 5, steps, 4 - steps)) & 7
    native = ((source >> 1) & 1) == xh
    origin = jnp.where(native, source, (source + 2 * (source & 1) - 1) & 7)
    slab = jnp.where(native, xh, 1 - xh)
    place = jnp.stack([(origin >> 2) * 2 + (origin & 1), slab ^ xh, slab]).astype(jnp.int32)
    own_weight, sent_weight = assemble(
        place, home, first, second, third, *exchanged, last, swap(last, "core")
    )

    tables = rope_tables(seq_rows, head_size)
    gain_row = lax.dynamic_slice_in_dim(key_gain, z, 1, 0)
    cut = seq_rows // 3 * 2

    def product(rows, weight):
        return lax.dot_general(rows, weight, (((0,), (0,)), ((), ())), preferred_element_type=jnp.float32)

    tokens = [normed[:, :cut], normed[:, cut:]]
    got = [swap(product(rows, sent_weight).astype(jnp.bfloat16), "xh") for rows in tokens]
    result = ()
    for rows, other in zip(tokens, got):
        own = product(rows, own_weight)
        result = attend(prompt_len, own, other, query_gain, gain_row, tables, tuple(result))
    return result[0]


def solution(mesh):
    fine = Mesh(mesh.devices.reshape(SIZES), AXES)
    rows, cols = ("xl", "core", "y"), ("z", "xh")
    slab = P(rows, cols, None, None)
    in_specs = (P(rows, cols), P(), slab, slab, slab, slab, P(cols, None), P(), P(rows))
    return jax.shard_map(
        shards, mesh=fine, in_specs=in_specs, out_specs=P(rows, cols), check_vma=False
    )
```

```python
import functools

import jax
import jax.numpy as jnp
import numpy as np
from jax import lax
from jax.experimental import pallas as pl
from jax.experimental.pallas import tpu as pltpu
from jax.sharding import Mesh, PartitionSpec as P

STEP_SCALE = 0.5
BETA_ONE = 0.9
BETA_TWO = 0.95
ROPE_BASE = 500000.0
AXES = ("xl", "core", "y", "z", "xh")
SIZES = (2, 2, 8, 8, 2)


def rope_tables(length, head_size):
    exponent = np.arange(head_size // 2, dtype=np.float32) * np.float32(2.0) / head_size
    inverse = np.power(np.float64(ROPE_BASE), -exponent.astype(np.float64)).astype(np.float32)
    angles = np.arange(length, dtype=np.float32)[:, None] * inverse[None, :]
    cosine = np.cos(angles.astype(np.float64)).astype(np.float32)
    sine = np.sin(angles.astype(np.float64)).astype(np.float32)
    return np.concatenate([cosine, cosine], axis=1), np.concatenate([-sine, sine], axis=1)


def rms_rotated(inputs, gain, cosine, sine):
    scale = lax.rsqrt(jnp.mean(inputs * inputs, axis=-1, keepdims=True) + 1e-06)
    scaled = inputs * scale * gain
    return scaled * cosine + pltpu.roll(scaled, scaled.shape[-1] // 2, 1) * sine


VMEM = pl.BlockSpec(memory_space=pltpu.VMEM)
SMEM = pl.BlockSpec(memory_space=pltpu.SMEM)


def local_call(kernel, name, out_shape, in_specs, out_specs):
    return pl.pallas_call(
        kernel,
        out_shape=out_shape,
        in_specs=in_specs,
        out_specs=out_specs,
        compiler_params=pltpu.CompilerParams(vmem_limit_bytes=8 << 20),
        name=name,
    )


def put_block(place_ref, step, lane, block_ref, index, own_ref, sent_ref):
    rows, cols = block_ref.shape[-2:]
    head = own_ref.shape[1] // 4
    wide = cols - head
    row = pl.multiple_of(place_ref[0, step] * rows, 32)
    pair_col = pl.multiple_of(wide + place_ref[2, step] * head, 128)
    spans = [pl.ds((lane * 2 + near) * 4 * rows + row, rows) for near in range(2)]

    def put_queries(out_ref):
        for near, span in enumerate(spans):
            out_ref[span, :wide] = block_ref[*index, near, :, :wide]

    pl.when(place_ref[1, step] == 0)(lambda: put_queries(own_ref))
    pl.when(place_ref[1, step] == 1)(lambda: put_queries(sent_ref))
    for near, span in enumerate(spans):
        pair = block_ref[*index, near, :, wide:]
        own_ref[span, pl.ds(pair_col, head)] = pair
        sent_ref[span, pl.ds(pair_col, head)] = pair


def assemble_kernel(place_ref, *refs):
    *block_refs, last_ref, final_ref, own_ref, sent_ref = refs
    outs = (own_ref, sent_ref)
    for lane in range(2):
        for step in range(4):
            put_block(place_ref, step, lane, block_refs[step], (lane,), *outs)
        for step in range(3):
            put_block(place_ref, 5 + step, 1 - lane, block_refs[4 + step], (lane,), *outs)
    put_block(place_ref, 4, 0, last_ref, (), *outs)
    put_block(place_ref, 4, 1, final_ref, (), *outs)


def assemble(place, home, *rest):
    _, _, rows, cols = home.shape
    shape = [jax.ShapeDtypeStruct((16 * rows, 4 * cols // 3), home.dtype)] * 2
    call = local_call(assemble_kernel, "assemble", shape, [SMEM] + [VMEM] * (1 + len(rest)), [VMEM] * 2)
    return call(place, home, *rest)


def squares_kernel(parts, features_ref, out_ref):
    rows = features_ref.shape[0] // parts
    total = None
    for step in range(parts):
        wide = features_ref[step * rows : (step + 1) * rows, :].astype(jnp.float32)
        square = jnp.sum(wide * wide, axis=0, keepdims=True)
        total = square if total is None else total + square
    out_ref[...] = total


def squares(parts, features):
    shape = jax.ShapeDtypeStruct((1, features.shape[1]), jnp.float32)
    return local_call(functools.partial(squares_kernel, parts), "squares", shape, [VMEM], VMEM)(features)


def normalise_kernel(width_all, parts, place_ref, square_ref, other_ref, gain_ref, features_ref, out_ref):
    rows = features_ref.shape[0] // parts
    scale = lax.rsqrt((square_ref[...] + other_ref[...]) / width_all + 1e-06)
    for step in range(parts):
        span = slice(step * rows, (step + 1) * rows)
        row = pl.multiple_of(place_ref[step] * rows, 64)
        scaled = features_ref[span, :].astype(jnp.float32) * scale * gain_ref[span, :]
        out_ref[pl.ds(row, rows), :] = scaled.astype(out_ref.dtype)


def normalise(width_all, parts, place, square, other, gain, features):
    shape = jax.ShapeDtypeStruct(features.shape, jnp.bfloat16)
    kernel = functools.partial(normalise_kernel, width_all, parts)
    call = local_call(kernel, "normalise", shape, [SMEM] + [VMEM] * 4, VMEM)
    return call(place, square, other, gain, features)


def attend_kernel(tile, first, limit_ref, own_ref, got_ref, query_gain_ref, key_gain_ref, cos_ref, sin_ref, *refs):
    before, out_ref, keys_ref, values_ref = refs[:-3], *refs[-3:]
    heads, head = query_gain_ref.shape
    wide = heads * head
    limit = limit_ref[0]
    rows = own_ref.shape[0]
    if before:
        out_ref[:first, :] = before[0][...]
        keys_ref[:first, :] = before[1][...]
        values_ref[:first, :] = before[2][...]

    def summed(start, size, col):
        got = got_ref[start : start + size, col : col + head].astype(jnp.float32)
        return own_ref[start : start + size, col : col + head] + got

    cosine, sine = cos_ref[first : first + rows, :], sin_ref[first : first + rows, :]
    keys = rms_rotated(summed(0, rows, wide), key_gain_ref[...], cosine, sine)
    keys_ref[first:, :] = keys.astype(jnp.bfloat16)
    values_ref[first:, :] = summed(0, rows, wide + head).astype(jnp.bfloat16)
    for start in range(0, rows, tile):
        seen = first + start + tile
        row = first + start + lax.broadcasted_iota(jnp.int32, (tile, seen), 0)
        col = lax.broadcasted_iota(jnp.int32, (tile, seen), 1)
        allowed = (col <= row) & (col < limit)
        cosine, sine = cos_ref[first + start : seen, :], sin_ref[first + start : seen, :]
        for j in range(heads):
            projected = summed(start, tile, j * head)
            query = rms_rotated(projected, query_gain_ref[j : j + 1, :], cosine, sine)
            query = (query * head**-0.5).astype(jnp.bfloat16)
            scores = lax.dot_general(
                query, keys_ref[:seen, :], (((1,), (1,)), ((), ())), preferred_element_type=jnp.float32
            )
            scores = jnp.where(allowed, scores, -1e30)
            weights = jnp.exp(scores - jnp.max(scores, axis=-1, keepdims=True))
            weights = weights * (1.0 / jnp.sum(weights, axis=-1, keepdims=True))
            output = jnp.dot(weights.astype(jnp.bfloat16), values_ref[:seen, :], preferred_element_type=jnp.float32)
            out_ref[first + start : seen, j * head : (j + 1) * head] = output.astype(out_ref.dtype)


def attend(limit, own, got, query_gain, key_gain, tables, before):
    rows = own.shape[0]
    heads, head = query_gain.shape
    first = before[0].shape[0] if before else 0
    shape = [jax.ShapeDtypeStruct((first + rows, n), jnp.bfloat16) for n in (heads * head, head, head)]
    kernel = functools.partial(attend_kernel, min(rows, 256), first)
    call = local_call(kernel, "attend", shape, [SMEM] + [VMEM] * (6 + len(before)), [VMEM] * 3)
    return call(limit, own, got, query_gain, key_gain, *tables, *before)


def swap(array, axis):
    return lax.ppermute(array, axis, [(0, 1), (1, 0)])


def global_sum(value):
    count = 1
    for size in SIZES:
        count *= size
    spread = jnp.broadcast_to(value, (count, 128))
    return jnp.sum(lax.all_to_all(spread, AXES, 0, 0, tiled=True)[:, 0])


def to_column(block, other):
    pairs = []
    for xl in range(2):
        for y in range(8):
            for slab in range(2):
                column = (y >> 1) % 2
                target = y if slab == column else (y + (1 if y % 2 else -1)) % 8
                pairs.append(((xl * 8 + y) * 2 + slab, ((xl ^ other) * 8 + target) * 2 + column))
    return lax.ppermute(block, ("xl", "y", "xh"), pairs)


def onward(block, steps):
    pairs = [(y, (y + steps) % 8) for y in range(8)] + [(8 + y, 8 + (y - steps) % 8) for y in range(8)]
    return lax.ppermute(block, ("core", "y"), pairs)


def shards(
    activations, norm_gain, master_weight, grad, moment, variance, query_gain, key_gain, prompt_len
):
    xl, core, y, z, xh = (lax.axis_index(a) for a in AXES)
    width_all = norm_gain.shape[0]
    seq_rows, width_part = activations.shape
    slab_rows, _, slab_heads, head_size = grad.shape
    steps = jnp.arange(8)

    gathered = lax.all_gather(activations.T, "z", axis=0, tiled=True)

    grad_local = grad.astype(jnp.float32)
    sumsq = global_sum(jnp.sum(grad_local * grad_local))
    flat = (slab_rows, slab_heads * head_size)
    flats = [array.reshape(flat) for array in (master_weight, moment, variance, grad)]
    gain = lax.dynamic_index_in_dim(norm_gain.reshape(8, 2, width_part), xh, 1, False).reshape(-1, 1)
    sumsq, gain, *flats = lax.optimization_barrier((sumsq, gain, *flats))
    master_flat, moment_flat, variance_flat, grad_flat = flats
    clip_factor = 1.0 / jnp.sqrt(sumsq + 1e-12)
    clipped = grad_flat.astype(jnp.float32) * clip_factor
    moment_new = BETA_ONE * moment_flat + (1.0 - BETA_ONE) * clipped
    variance_new = BETA_TWO * variance_flat + (1.0 - BETA_TWO) * clipped * clipped
    step_size = STEP_SCALE * width_all ** (-0.5)
    updated = (master_flat - step_size * moment_new / (jnp.sqrt(variance_new) + 1e-08)).astype(
        jnp.bfloat16
    )
    home = jnp.stack([to_column(updated, 0), to_column(updated, 1)])
    home = jnp.stack([home, swap(home, "core")])
    first, second = onward(home, 1), onward(home, 2)
    first, gathered = lax.optimization_barrier((first, gathered))
    square = squares(8, gathered)
    other_square = swap(square, "xh")
    second, other_square = lax.optimization_barrier((second, other_square))
    place = (((((steps >> 1) & 1) ^ core) * 2 + ((steps >> 2) ^ xl)) * 2 + (steps & 1)).astype(jnp.int32)
    normed = normalise(float(width_all), 8, place, square, other_square, gain, gathered)

    third, last = onward(second, 1), onward(second[0], 2)
    third, normed = lax.optimization_barrier((third, normed))
    exchanged = [swap(block, "core") for block in (first, second, third)]

    up = 1 - 2 * core
    source = (y - up * jnp.where(steps < 5, steps, 4 - steps)) & 7
    native = ((source >> 1) & 1) == xh
    origin = jnp.where(native, source, (source + 2 * (source & 1) - 1) & 7)
    slab = jnp.where(native, xh, 1 - xh)
    place = jnp.stack([(origin >> 2) * 2 + (origin & 1), slab ^ xh, slab]).astype(jnp.int32)
    own_weight, sent_weight = assemble(
        place, home, first, second, third, *exchanged, last, swap(last, "core")
    )

    tables = rope_tables(seq_rows, head_size)
    gain_row = lax.dynamic_slice_in_dim(key_gain, z, 1, 0)
    cut = seq_rows // 3 * 2

    def product(rows, weight):
        return lax.dot_general(rows, weight, (((0,), (0,)), ((), ())), preferred_element_type=jnp.float32)

    tokens = [normed[:, :cut], normed[:, cut:]]
    got = [swap(product(rows, sent_weight).astype(jnp.bfloat16), "xh") for rows in tokens]
    result = ()
    for rows, other in zip(tokens, got):
        own = product(rows, own_weight)
        result = attend(prompt_len, own, other, query_gain, gain_row, tables, tuple(result))
    return result[0]


def solution(mesh):
    fine = Mesh(mesh.devices.reshape(SIZES), AXES)
    rows, cols = ("xl", "core", "y"), ("z", "xh")
    slab = P(rows, cols, None, None)
    in_specs = (P(rows, cols), P(), slab, slab, slab, slab, P(cols, None), P(), P(rows))
    return jax.shard_map(
        shards, mesh=fine, in_specs=in_specs, out_specs=P(rows, cols), check_vma=False
    )
```

```python
import functools

import jax
import jax.numpy as jnp
import numpy as np
from jax import lax
from jax.experimental import pallas as pl
from jax.experimental.pallas import tpu as pltpu
from jax.sharding import Mesh, PartitionSpec as P

STEP_SCALE = 0.5
BETA_ONE = 0.9
BETA_TWO = 0.95
ROPE_BASE = 500000.0
AXES = ("xl", "core", "y", "z", "xh")
SIZES = (2, 2, 8, 8, 2)


def rope_tables(length, head_size):
    exponent = np.arange(head_size // 2, dtype=np.float32) * np.float32(2.0) / head_size
    inverse = np.power(np.float64(ROPE_BASE), -exponent.astype(np.float64)).astype(np.float32)
    angles = np.arange(length, dtype=np.float32)[:, None] * inverse[None, :]
    cosine = np.cos(angles.astype(np.float64)).astype(np.float32)
    sine = np.sin(angles.astype(np.float64)).astype(np.float32)
    return np.concatenate([cosine, cosine], axis=1), np.concatenate([-sine, sine], axis=1)


def rms_rotated(inputs, gain, cosine, sine):
    scale = lax.rsqrt(jnp.mean(inputs * inputs, axis=-1, keepdims=True) + 1e-06)
    scaled = inputs * scale * gain
    return scaled * cosine + pltpu.roll(scaled, scaled.shape[-1] // 2, 1) * sine


VMEM = pl.BlockSpec(memory_space=pltpu.VMEM)
SMEM = pl.BlockSpec(memory_space=pltpu.SMEM)


def local_call(kernel, name, out_shape, in_specs, out_specs):
    return pl.pallas_call(
        kernel,
        out_shape=out_shape,
        in_specs=in_specs,
        out_specs=out_specs,
        compiler_params=pltpu.CompilerParams(vmem_limit_bytes=8 << 20),
        name=name,
    )


def put_block(place_ref, step, lane, block_ref, index, own_ref, sent_ref):
    rows, cols = block_ref.shape[-2:]
    head = own_ref.shape[1] // 4
    wide = cols - head
    row = pl.multiple_of(place_ref[0, step] * rows, 32)
    pair_col = pl.multiple_of(wide + place_ref[2, step] * head, 128)
    spans = [pl.ds((lane * 2 + near) * 4 * rows + row, rows) for near in range(2)]

    def put_queries(out_ref):
        for near, span in enumerate(spans):
            out_ref[span, :wide] = block_ref[*index, near, :, :wide]

    pl.when(place_ref[1, step] == 0)(lambda: put_queries(own_ref))
    pl.when(place_ref[1, step] == 1)(lambda: put_queries(sent_ref))
    for near, span in enumerate(spans):
        pair = block_ref[*index, near, :, wide:]
        own_ref[span, pl.ds(pair_col, head)] = pair
        sent_ref[span, pl.ds(pair_col, head)] = pair


def assemble_kernel(place_ref, *refs):
    *block_refs, last_ref, final_ref, own_ref, sent_ref = refs
    outs = (own_ref, sent_ref)
    for lane in range(2):
        for step in range(4):
            put_block(place_ref, step, lane, block_refs[step], (lane,), *outs)
        for step in range(3):
            put_block(place_ref, 5 + step, 1 - lane, block_refs[4 + step], (lane,), *outs)
    put_block(place_ref, 4, 0, last_ref, (), *outs)
    put_block(place_ref, 4, 1, final_ref, (), *outs)


def assemble(place, home, *rest):
    _, _, rows, cols = home.shape
    shape = [jax.ShapeDtypeStruct((16 * rows, 4 * cols // 3), home.dtype)] * 2
    call = local_call(assemble_kernel, "assemble", shape, [SMEM] + [VMEM] * (1 + len(rest)), [VMEM] * 2)
    return call(place, home, *rest)


def squares_kernel(features_ref, out_ref):
    wide = features_ref[...].astype(jnp.float32)
    square = jnp.sum(wide * wide, axis=0, keepdims=True)

    @pl.when(pl.program_id(0) == 0)
    def _():
        out_ref[...] = square

    @pl.when(pl.program_id(0) > 0)
    def _():
        out_ref[...] += square


def squares(parts, features):
    rows, cols = features.shape[0] // parts, features.shape[1]
    return pl.pallas_call(
        squares_kernel,
        grid=(parts,),
        out_shape=jax.ShapeDtypeStruct((1, cols), jnp.float32),
        in_specs=[pl.BlockSpec((rows, cols), lambda i: (i, 0))],
        out_specs=pl.BlockSpec((1, cols), lambda i: (0, 0)),
        compiler_params=pltpu.CompilerParams(vmem_limit_bytes=8 << 20),
        name="squares",
    )(features)


def normalise_kernel(width_all, place_ref, square_ref, other_ref, gain_ref, features_ref, out_ref):
    scale = lax.rsqrt((square_ref[...] + other_ref[...]) / width_all + 1e-06)
    scaled = features_ref[...].astype(jnp.float32) * scale * gain_ref[...]
    out_ref[...] = scaled.astype(out_ref.dtype)


def normalise(width_all, parts, place, square, other, gain, features):
    rows, cols = features.shape[0] // parts, features.shape[1]
    whole = pl.BlockSpec((1, cols), lambda i, place: (0, 0))
    grid_spec = pltpu.PrefetchScalarGridSpec(
        num_scalar_prefetch=1,
        grid=(parts,),
        in_specs=[
            whole,
            whole,
            pl.BlockSpec((rows, 1), lambda i, place: (i, 0)),
            pl.BlockSpec((rows, cols), lambda i, place: (i, 0)),
        ],
        out_specs=pl.BlockSpec((rows, cols), lambda i, place: (place[i], 0)),
    )
    return pl.pallas_call(
        functools.partial(normalise_kernel, width_all),
        grid_spec=grid_spec,
        out_shape=jax.ShapeDtypeStruct(features.shape, jnp.bfloat16),
        compiler_params=pltpu.CompilerParams(vmem_limit_bytes=8 << 20),
        name="normalise",
    )(place, square, other, gain, features)


def attend_kernel(tile, first, limit_ref, own_ref, got_ref, query_gain_ref, key_gain_ref, cos_ref, sin_ref, *refs):
    before, out_ref, keys_ref, values_ref = refs[:-3], *refs[-3:]
    heads, head = query_gain_ref.shape
    wide = heads * head
    limit = limit_ref[0]
    rows = own_ref.shape[0]
    if before:
        out_ref[:first, :] = before[0][...]
        keys_ref[:first, :] = before[1][...]
        values_ref[:first, :] = before[2][...]

    def summed(start, size, col):
        got = got_ref[start : start + size, col : col + head].astype(jnp.float32)
        return own_ref[start : start + size, col : col + head] + got

    cosine, sine = cos_ref[first : first + rows, :], sin_ref[first : first + rows, :]
    keys = rms_rotated(summed(0, rows, wide), key_gain_ref[...], cosine, sine)
    keys_ref[first:, :] = keys.astype(jnp.bfloat16)
    values_ref[first:, :] = summed(0, rows, wide + head).astype(jnp.bfloat16)
    for start in range(0, rows, tile):
        seen = first + start + tile
        row = first + start + lax.broadcasted_iota(jnp.int32, (tile, seen), 0)
        col = lax.broadcasted_iota(jnp.int32, (tile, seen), 1)
        allowed = (col <= row) & (col < limit)
        cosine, sine = cos_ref[first + start : seen, :], sin_ref[first + start : seen, :]
        for j in range(heads):
            projected = summed(start, tile, j * head)
            query = rms_rotated(projected, query_gain_ref[j : j + 1, :], cosine, sine)
            query = (query * head**-0.5).astype(jnp.bfloat16)
            scores = lax.dot_general(
                query, keys_ref[:seen, :], (((1,), (1,)), ((), ())), preferred_element_type=jnp.float32
            )
            scores = jnp.where(allowed, scores, -1e30)
            weights = jnp.exp(scores - jnp.max(scores, axis=-1, keepdims=True))
            weights = weights * (1.0 / jnp.sum(weights, axis=-1, keepdims=True))
            output = jnp.dot(weights.astype(jnp.bfloat16), values_ref[:seen, :], preferred_element_type=jnp.float32)
            out_ref[first + start : seen, j * head : (j + 1) * head] = output.astype(out_ref.dtype)


def attend(limit, own, got, query_gain, key_gain, tables, before):
    rows = own.shape[0]
    heads, head = query_gain.shape
    first = before[0].shape[0] if before else 0
    shape = [jax.ShapeDtypeStruct((first + rows, n), jnp.bfloat16) for n in (heads * head, head, head)]
    kernel = functools.partial(attend_kernel, min(rows, 256), first)
    call = local_call(kernel, "attend", shape, [SMEM] + [VMEM] * (6 + len(before)), [VMEM] * 3)
    return call(limit, own, got, query_gain, key_gain, *tables, *before)


def swap(array, axis):
    return lax.ppermute(array, axis, [(0, 1), (1, 0)])


def global_sum(value):
    count = 1
    for size in SIZES:
        count *= size
    spread = jnp.broadcast_to(value, (count, 128))
    return jnp.sum(lax.all_to_all(spread, AXES, 0, 0, tiled=True)[:, 0])


def to_column(block, other):
    pairs = []
    for xl in range(2):
        for y in range(8):
            for slab in range(2):
                column = (y >> 1) % 2
                target = y if slab == column else (y + (1 if y % 2 else -1)) % 8
                pairs.append(((xl * 8 + y) * 2 + slab, ((xl ^ other) * 8 + target) * 2 + column))
    return lax.ppermute(block, ("xl", "y", "xh"), pairs)


def onward(block, steps):
    pairs = [(y, (y + steps) % 8) for y in range(8)] + [(8 + y, 8 + (y - steps) % 8) for y in range(8)]
    return lax.ppermute(block, ("core", "y"), pairs)


def shards(
    activations, norm_gain, master_weight, grad, moment, variance, query_gain, key_gain, prompt_len
):
    xl, core, y, z, xh = (lax.axis_index(a) for a in AXES)
    width_all = norm_gain.shape[0]
    seq_rows, width_part = activations.shape
    slab_rows, _, slab_heads, head_size = grad.shape
    steps = jnp.arange(8)

    gathered = lax.all_gather(activations.T, "z", axis=0, tiled=True)

    grad_local = grad.astype(jnp.float32)
    sumsq = global_sum(jnp.sum(grad_local * grad_local))
    flat = (slab_rows, slab_heads * head_size)
    flats = [array.reshape(flat) for array in (master_weight, moment, variance, grad)]
    gain = lax.dynamic_index_in_dim(norm_gain.reshape(8, 2, width_part), xh, 1, False).reshape(-1, 1)
    sumsq, gain, *flats = lax.optimization_barrier((sumsq, gain, *flats))
    master_flat, moment_flat, variance_flat, grad_flat = flats
    clip_factor = 1.0 / jnp.sqrt(sumsq + 1e-12)
    clipped = grad_flat.astype(jnp.float32) * clip_factor
    moment_new = BETA_ONE * moment_flat + (1.0 - BETA_ONE) * clipped
    variance_new = BETA_TWO * variance_flat + (1.0 - BETA_TWO) * clipped * clipped
    step_size = STEP_SCALE * width_all ** (-0.5)
    updated = (master_flat - step_size * moment_new / (jnp.sqrt(variance_new) + 1e-08)).astype(
        jnp.bfloat16
    )
    home = jnp.stack([to_column(updated, 0), to_column(updated, 1)])
    home = jnp.stack([home, swap(home, "core")])
    first, second = onward(home, 1), onward(home, 2)
    first, gathered = lax.optimization_barrier((first, gathered))
    exchanged = [swap(first, "core")]

    square = squares(8, gathered)
    second, square, exchanged[0] = lax.optimization_barrier((second, square, exchanged[0]))
    other_square = swap(square, "xh")
    place = (((((steps >> 1) & 1) ^ core) * 2 + ((steps >> 2) ^ xl)) * 2 + (steps & 1)).astype(jnp.int32)
    normed = normalise(float(width_all), 8, place, square, other_square, gain, gathered)

    third, last = onward(second, 1), onward(second[0], 2)
    third, normed = lax.optimization_barrier((third, normed))
    exchanged += [swap(second, "core"), swap(third, "core")]

    up = 1 - 2 * core
    source = (y - up * jnp.where(steps < 5, steps, 4 - steps)) & 7
    native = ((source >> 1) & 1) == xh
    origin = jnp.where(native, source, (source + 2 * (source & 1) - 1) & 7)
    slab = jnp.where(native, xh, 1 - xh)
    place = jnp.stack([(origin >> 2) * 2 + (origin & 1), slab ^ xh, slab]).astype(jnp.int32)
    own_weight, sent_weight = assemble(
        place, home, first, second, third, *exchanged, last, swap(last, "core")
    )

    tables = rope_tables(seq_rows, head_size)
    gain_row = lax.dynamic_slice_in_dim(key_gain, z, 1, 0)
    cut = seq_rows // 3 * 2

    def product(rows, weight):
        return lax.dot_general(rows, weight, (((0,), (0,)), ((), ())), preferred_element_type=jnp.float32)

    tokens = [normed[:, :cut], normed[:, cut:]]
    got = [swap(product(rows, sent_weight).astype(jnp.bfloat16), "xh") for rows in tokens]
    result = ()
    for rows, other in zip(tokens, got):
        own = product(rows, own_weight)
        result = attend(prompt_len, own, other, query_gain, gain_row, tables, tuple(result))
    return result[0]


def solution(mesh):
    fine = Mesh(mesh.devices.reshape(SIZES), AXES)
    rows, cols = ("xl", "core", "y"), ("z", "xh")
    slab = P(rows, cols, None, None)
    in_specs = (P(rows, cols), P(), slab, slab, slab, slab, P(cols, None), P(), P(rows))
    return jax.shard_map(
        shards, mesh=fine, in_specs=in_specs, out_specs=P(rows, cols), check_vma=False
    )
```

```python
import functools

import jax
import jax.numpy as jnp
import numpy as np
from jax import lax
from jax.experimental import pallas as pl
from jax.experimental.pallas import tpu as pltpu
from jax.sharding import Mesh, PartitionSpec as P

STEP_SCALE = 0.5
BETA_ONE = 0.9
BETA_TWO = 0.95
ROPE_BASE = 500000.0
AXES = ("xl", "core", "y", "z", "xh")
SIZES = (2, 2, 8, 8, 2)


def rope_tables(length, head_size):
    exponent = np.arange(head_size // 2, dtype=np.float32) * np.float32(2.0) / head_size
    inverse = np.power(np.float64(ROPE_BASE), -exponent.astype(np.float64)).astype(np.float32)
    angles = np.arange(length, dtype=np.float32)[:, None] * inverse[None, :]
    cosine = np.cos(angles.astype(np.float64)).astype(np.float32)
    sine = np.sin(angles.astype(np.float64)).astype(np.float32)
    return np.concatenate([cosine, cosine], axis=1), np.concatenate([-sine, sine], axis=1)


def rms_rotated(inputs, gain, cosine, sine):
    scale = lax.rsqrt(jnp.mean(inputs * inputs, axis=-1, keepdims=True) + 1e-06)
    scaled = inputs * scale * gain
    return scaled * cosine + pltpu.roll(scaled, scaled.shape[-1] // 2, 1) * sine


VMEM = pl.BlockSpec(memory_space=pltpu.VMEM)
SMEM = pl.BlockSpec(memory_space=pltpu.SMEM)


def local_call(kernel, name, out_shape, in_specs, out_specs):
    return pl.pallas_call(
        kernel,
        out_shape=out_shape,
        in_specs=in_specs,
        out_specs=out_specs,
        compiler_params=pltpu.CompilerParams(vmem_limit_bytes=8 << 20),
        name=name,
    )


def put_block(place_ref, step, lane, block_ref, index, own_ref, sent_ref):
    rows, cols = block_ref.shape[-2:]
    head = own_ref.shape[1] // 4
    wide = cols - head
    row = pl.multiple_of(place_ref[0, step] * rows, 32)
    pair_col = pl.multiple_of(wide + place_ref[2, step] * head, 128)
    spans = [pl.ds((lane * 2 + near) * 4 * rows + row, rows) for near in range(2)]

    def put_queries(out_ref):
        for near, span in enumerate(spans):
            out_ref[span, :wide] = block_ref[*index, near, :, :wide]

    pl.when(place_ref[1, step] == 0)(lambda: put_queries(own_ref))
    pl.when(place_ref[1, step] == 1)(lambda: put_queries(sent_ref))
    for near, span in enumerate(spans):
        pair = block_ref[*index, near, :, wide:]
        own_ref[span, pl.ds(pair_col, head)] = pair
        sent_ref[span, pl.ds(pair_col, head)] = pair


def assemble_kernel(place_ref, *refs):
    *block_refs, last_ref, final_ref, own_ref, sent_ref = refs
    outs = (own_ref, sent_ref)
    for lane in range(2):
        for step in range(4):
            put_block(place_ref, step, lane, block_refs[step], (lane,), *outs)
        for step in range(3):
            put_block(place_ref, 5 + step, 1 - lane, block_refs[4 + step], (lane,), *outs)
    put_block(place_ref, 4, 0, last_ref, (), *outs)
    put_block(place_ref, 4, 1, final_ref, (), *outs)


def assemble(place, home, *rest):
    _, _, rows, cols = home.shape
    shape = [jax.ShapeDtypeStruct((16 * rows, 4 * cols // 3), home.dtype)] * 2
    call = local_call(assemble_kernel, "assemble", shape, [SMEM] + [VMEM] * (1 + len(rest)), [VMEM] * 2)
    return call(place, home, *rest)


def squares_kernel(features_ref, out_ref):
    wide = features_ref[...].astype(jnp.float32)
    square = jnp.sum(wide * wide, axis=0, keepdims=True)

    @pl.when(pl.program_id(0) == 0)
    def _():
        out_ref[...] = square

    @pl.when(pl.program_id(0) > 0)
    def _():
        out_ref[...] += square


def squares(parts, features):
    rows, cols = features.shape[0] // parts, features.shape[1]
    return pl.pallas_call(
        squares_kernel,
        grid=(parts,),
        out_shape=jax.ShapeDtypeStruct((1, cols), jnp.float32),
        in_specs=[pl.BlockSpec((rows, cols), lambda i: (i, 0))],
        out_specs=pl.BlockSpec((1, cols), lambda i: (0, 0)),
        compiler_params=pltpu.CompilerParams(vmem_limit_bytes=8 << 20),
        name="squares",
    )(features)


def normalise_kernel(width_all, place_ref, square_ref, other_ref, gain_ref, features_ref, out_ref):
    scale = lax.rsqrt((square_ref[...] + other_ref[...]) / width_all + 1e-06)
    scaled = features_ref[...].astype(jnp.float32) * scale * gain_ref[...]
    out_ref[...] = scaled.astype(out_ref.dtype)


def normalise(width_all, parts, place, square, other, gain, features):
    rows, cols = features.shape[0] // parts, features.shape[1]
    whole = pl.BlockSpec((1, cols), lambda i, place: (0, 0))
    grid_spec = pltpu.PrefetchScalarGridSpec(
        num_scalar_prefetch=1,
        grid=(parts,),
        in_specs=[
            whole,
            whole,
            pl.BlockSpec((rows, 1), lambda i, place: (i, 0)),
            pl.BlockSpec((rows, cols), lambda i, place: (i, 0)),
        ],
        out_specs=pl.BlockSpec((rows, cols), lambda i, place: (place[i], 0)),
    )
    return pl.pallas_call(
        functools.partial(normalise_kernel, width_all),
        grid_spec=grid_spec,
        out_shape=pltpu.HBM(features.shape, jnp.bfloat16),
        compiler_params=pltpu.CompilerParams(vmem_limit_bytes=8 << 20),
        name="normalise",
    )(place, square, other, gain, features)


def attend_kernel(tile, first, limit_ref, own_ref, got_ref, query_gain_ref, key_gain_ref, cos_ref, sin_ref, *refs):
    before, out_ref, keys_ref, values_ref = refs[:-3], *refs[-3:]
    heads, head = query_gain_ref.shape
    wide = heads * head
    limit = limit_ref[0]
    rows = own_ref.shape[0]
    if before:
        out_ref[:first, :] = before[0][...]
        keys_ref[:first, :] = before[1][...]
        values_ref[:first, :] = before[2][...]

    def summed(start, size, col):
        got = got_ref[start : start + size, col : col + head].astype(jnp.float32)
        return own_ref[start : start + size, col : col + head] + got

    cosine, sine = cos_ref[first : first + rows, :], sin_ref[first : first + rows, :]
    keys = rms_rotated(summed(0, rows, wide), key_gain_ref[...], cosine, sine)
    keys_ref[first:, :] = keys.astype(jnp.bfloat16)
    values_ref[first:, :] = summed(0, rows, wide + head).astype(jnp.bfloat16)
    for start in range(0, rows, tile):
        seen = first + start + tile
        row = first + start + lax.broadcasted_iota(jnp.int32, (tile, seen), 0)
        col = lax.broadcasted_iota(jnp.int32, (tile, seen), 1)
        allowed = (col <= row) & (col < limit)
        cosine, sine = cos_ref[first + start : seen, :], sin_ref[first + start : seen, :]
        for j in range(heads):
            projected = summed(start, tile, j * head)
            query = rms_rotated(projected, query_gain_ref[j : j + 1, :], cosine, sine)
            query = (query * head**-0.5).astype(jnp.bfloat16)
            scores = lax.dot_general(
                query, keys_ref[:seen, :], (((1,), (1,)), ((), ())), preferred_element_type=jnp.float32
            )
            scores = jnp.where(allowed, scores, -1e30)
            weights = jnp.exp(scores - jnp.max(scores, axis=-1, keepdims=True))
            weights = weights * (1.0 / jnp.sum(weights, axis=-1, keepdims=True))
            output = jnp.dot(weights.astype(jnp.bfloat16), values_ref[:seen, :], preferred_element_type=jnp.float32)
            out_ref[first + start : seen, j * head : (j + 1) * head] = output.astype(out_ref.dtype)


def attend(limit, own, got, query_gain, key_gain, tables, before):
    rows = own.shape[0]
    heads, head = query_gain.shape
    first = before[0].shape[0] if before else 0
    shape = [jax.ShapeDtypeStruct((first + rows, n), jnp.bfloat16) for n in (heads * head, head, head)]
    kernel = functools.partial(attend_kernel, min(rows, 256), first)
    call = local_call(kernel, "attend", shape, [SMEM] + [VMEM] * (6 + len(before)), [VMEM] * 3)
    return call(limit, own, got, query_gain, key_gain, *tables, *before)


def swap(array, axis):
    return lax.ppermute(array, axis, [(0, 1), (1, 0)])


def global_sum(value):
    count = 1
    for size in SIZES:
        count *= size
    spread = jnp.broadcast_to(value, (count, 128))
    return jnp.sum(lax.all_to_all(spread, AXES, 0, 0, tiled=True)[:, 0])


def to_column(block, other):
    pairs = []
    for xl in range(2):
        for y in range(8):
            for slab in range(2):
                column = (y >> 1) % 2
                target = y if slab == column else (y + (1 if y % 2 else -1)) % 8
                pairs.append(((xl * 8 + y) * 2 + slab, ((xl ^ other) * 8 + target) * 2 + column))
    return lax.ppermute(block, ("xl", "y", "xh"), pairs)


def onward(block, steps):
    pairs = [(y, (y + steps) % 8) for y in range(8)] + [(8 + y, 8 + (y - steps) % 8) for y in range(8)]
    return lax.ppermute(block, ("core", "y"), pairs)


def shards(
    activations, norm_gain, master_weight, grad, moment, variance, query_gain, key_gain, prompt_len
):
    xl, core, y, z, xh = (lax.axis_index(a) for a in AXES)
    width_all = norm_gain.shape[0]
    seq_rows, width_part = activations.shape
    slab_rows, _, slab_heads, head_size = grad.shape
    steps = jnp.arange(8)

    gathered = lax.all_gather(activations.T, "z", axis=0, tiled=True)

    grad_local = grad.astype(jnp.float32)
    sumsq = global_sum(jnp.sum(grad_local * grad_local))
    flat = (slab_rows, slab_heads * head_size)
    flats = [array.reshape(flat) for array in (master_weight, moment, variance, grad)]
    gain = lax.dynamic_index_in_dim(norm_gain.reshape(8, 2, width_part), xh, 1, False).reshape(-1, 1)
    sumsq, gain, *flats = lax.optimization_barrier((sumsq, gain, *flats))
    master_flat, moment_flat, variance_flat, grad_flat = flats
    clip_factor = 1.0 / jnp.sqrt(sumsq + 1e-12)
    clipped = grad_flat.astype(jnp.float32) * clip_factor
    moment_new = BETA_ONE * moment_flat + (1.0 - BETA_ONE) * clipped
    variance_new = BETA_TWO * variance_flat + (1.0 - BETA_TWO) * clipped * clipped
    step_size = STEP_SCALE * width_all ** (-0.5)
    updated = (master_flat - step_size * moment_new / (jnp.sqrt(variance_new) + 1e-08)).astype(
        jnp.bfloat16
    )
    home = jnp.stack([to_column(updated, 0), to_column(updated, 1)])
    home = jnp.stack([home, swap(home, "core")])
    first, second = onward(home, 1), onward(home, 2)
    first, gathered = lax.optimization_barrier((first, gathered))
    exchanged = [swap(first, "core")]

    gathered = pltpu.with_memory_space_constraint(gathered, pltpu.HBM)
    square = squares(8, gathered)
    other_square = swap(square, "xh")
    second, other_square, exchanged[0] = lax.optimization_barrier((second, other_square, exchanged[0]))
    place = (((((steps >> 1) & 1) ^ core) * 2 + ((steps >> 2) ^ xl)) * 2 + (steps & 1)).astype(jnp.int32)
    normed = normalise(float(width_all), 8, place, square, other_square, gain, gathered)

    third, last = onward(second, 1), onward(second[0], 2)
    third, normed = lax.optimization_barrier((third, normed))
    exchanged += [swap(second, "core"), swap(third, "core")]

    up = 1 - 2 * core
    source = (y - up * jnp.where(steps < 5, steps, 4 - steps)) & 7
    native = ((source >> 1) & 1) == xh
    origin = jnp.where(native, source, (source + 2 * (source & 1) - 1) & 7)
    slab = jnp.where(native, xh, 1 - xh)
    place = jnp.stack([(origin >> 2) * 2 + (origin & 1), slab ^ xh, slab]).astype(jnp.int32)
    own_weight, sent_weight = assemble(
        place, home, first, second, third, *exchanged, last, swap(last, "core")
    )

    tables = rope_tables(seq_rows, head_size)
    gain_row = lax.dynamic_slice_in_dim(key_gain, z, 1, 0)
    cut = seq_rows // 3 * 2

    def product(rows, weight):
        return lax.dot_general(rows, weight, (((0,), (0,)), ((), ())), preferred_element_type=jnp.float32)

    tokens = [normed[:, :cut], normed[:, cut:]]
    got = [swap(product(rows, sent_weight).astype(jnp.bfloat16), "xh") for rows in tokens]
    result = ()
    for rows, other in zip(tokens, got):
        own = product(rows, own_weight)
        result = attend(prompt_len, own, other, query_gain, gain_row, tables, tuple(result))
    return result[0]


def solution(mesh):
    fine = Mesh(mesh.devices.reshape(SIZES), AXES)
    rows, cols = ("xl", "core", "y"), ("z", "xh")
    slab = P(rows, cols, None, None)
    in_specs = (P(rows, cols), P(), slab, slab, slab, slab, P(cols, None), P(), P(rows))
    return jax.shard_map(
        shards, mesh=fine, in_specs=in_specs, out_specs=P(rows, cols), check_vma=False
    )
```
